32 devices in a mesh: dp: 8 (over z, core), ctx: 4 (over y, x).
Axes of the slice: x: 2, y: 2, z: 4, core: 2. Of those that a mesh axis runs over, the one named last changes fastest.
Arguments:
- layer_input: bfloat16 [8, 512, 8192], P('dp', 'ctx'), may hold values from -6 to 6
- queries: bfloat16 [8, 512, 1024], P('dp', 'ctx'), may hold values from -68 to 68
- key_rows: bfloat16 [8, 512, 128], P('dp', 'ctx'), may hold values from -4 to 4
- value_rows: bfloat16 [8, 512, 128], P('dp', 'ctx'), may hold values from -5 to 5
- grad_output: bfloat16 [8, 512, 1024], P('dp', 'ctx'), may hold values from -12 to 12
- segments: int32 [8, 512], P('dp'), may hold values from 0 to 2, never falling along the last dimension, each value on 1 to 256 neighbouring positions
- lengths: int32 [8], P('dp'), may hold values from 256 to 512, as said below
Outputs:
- grad_queries: bfloat16 [8, 512, 1024], P('dp', 'ctx')
- grad_weights: bfloat16 [8192, 256], P(('dp', 'ctx'))
The draws below stay inside these ranges and needn't reach their ends.
Inputs may be any that keep to these rules, and one draw needn't show every extreme that they name: `lengths`: some rollout has all 512 positions live.
All inputs are finite; a program needn't handle non-finite values.
Results may differ from the reference program's by a relative error of at most 0.0057.
Values may be sent and summed in bfloat16 or wider, within the bound.
A program may use at most 64 MiB of HBM per device.

```python
import math
import jax
import jax.numpy as jnp
import numpy as np
from jax import lax

D = 8192
HD = 128
GROUP = 8
ROWS = 128
DOCS = 3
SPAN = 2
WINDOW = 256
SEQ = 512
ROLLOUTS = 8
N_DP = 8
N_CTX = 4


def shared_base(key):
    key_base = jnp.clip(jax.random.normal(jax.random.fold_in(key, 11), (ROLLOUTS, SEQ, HD), jnp.float32), -4.0, 4.0)
    return key_base


def draw_key_rows(key, part):
    key_base = shared_base(key)
    return key_base.astype(jnp.bfloat16)


def draw_queries(key, part):
    query_base = jnp.clip(jax.random.normal(jax.random.fold_in(key, 13), (ROLLOUTS, SEQ, GROUP * HD), jnp.float32), -4.0, 4.0)
    return query_base.astype(jnp.bfloat16)


def draw_lengths(key, part):
    picked = jax.random.randint(jax.random.fold_in(key, 21), (ROLLOUTS,), SEQ // 2, SEQ + 1)
    full_one = jax.random.randint(jax.random.fold_in(key, 22), (), 0, ROLLOUTS)
    return jnp.where(jnp.arange(ROLLOUTS) == full_one, SEQ, picked).astype(jnp.int32)


def strengthened(array, key, source, target, parts, factor):
    def block_of(position):
        return (jnp.arange(array.shape[position]) // (array.shape[position] // parts)).reshape((-1,) + (1,) * (array.ndim - 1 - position))

    one_side = jax.random.permutation(key, parts)[block_of(target)]
    far = (block_of(target) + parts // 2) % parts
    return jnp.where((block_of(source) == one_side) | (block_of(source) == far), factor * array, array)


def block_levels(stream_key, shape, cuts, low, high):
    level = 1.0
    for axis_at, shards_of in cuts:
        heights = jax.random.uniform(jax.random.fold_in(jax.random.fold_in(stream_key, 6), axis_at), (shards_of,), jnp.float32, low / len(cuts), high / len(cuts))
        level = level * jnp.repeat(jnp.exp(heights), shape[axis_at] // shards_of).reshape((-1,) + (1,) * (len(shape) - 1 - axis_at))
    return level


def length_profile(amount, total, most, lean):
    portions = [(1 << 20) // math.isqrt(standing ** lean) + 1 for standing in range(2, amount + 1)]
    rest, counts = total - most - (amount - 1), [1] * (amount - 1)
    while rest > 0:
        free = [i for i in range(amount - 1) if counts[i] < most]
        mass, budget = sum([portions[i] for i in free]), rest
        for i in free:
            extra = min(most - counts[i], max(1, budget * portions[i] // mass), rest)
            counts[i] = counts[i] + extra
            rest = rest - extra
    return np.array([most] + counts)


def uneven_parts(stream_key, amount, total, reach, skew):
    if amount == 2:
        one = jax.random.randint(stream_key, (), max(1, total - reach), min(reach, total - 1) + 1)
        return jnp.stack([one, total - one])
    sizes = jnp.asarray(length_profile(amount, total, reach, skew), jnp.int32)
    twos = (amount - 1) // 2
    giver, sink = sizes[1:1 + 2 * twos:2], sizes[2:2 + 2 * twos:2]
    margin = jnp.minimum(giver - 1, reach - sink)
    passed = jax.random.randint(jax.random.fold_in(stream_key, 1), (twos,), 0, 1 << 20) % (margin + 1)
    sizes = sizes.at[1:1 + 2 * twos:2].set(giver - passed).at[2:2 + 2 * twos:2].set(sink + passed)
    return sizes[jax.random.permutation(jax.random.fold_in(stream_key, 2), amount)]


def normal_values(key, shape, deviation, most, split=(), kind=jnp.bfloat16):
    entries = jax.random.normal(key, shape, jnp.float32) * deviation
    if len(split) > 0:
        entries = block_levels(key, shape, split, -0.22, 0.18) * entries
    return jnp.clip(entries, min=-most, max=most).astype(kind)


def heavy_noise(rng, shape, spread, reach, split, heavy, held_as=jnp.bfloat16):
    result = spread * jax.random.normal(rng, shape, jnp.float32)
    if split:
        result = result * block_levels(rng, shape, split, -0.22, 0.18)
    return jnp.clip(strengthened(result, jax.random.fold_in(rng, 3), *heavy), -reach, reach).astype(held_as)


def setup_inputs(seed: int = 0) -> dict:
    streams_of = jax.random.split(jax.random.key(seed), 8)
    layer_input = heavy_noise(streams_of[0], (ROLLOUTS, SEQ, D), 1.0, 6.0, ((0, 8), (1, 4)), (0, 2, 8, 2.0))
    queries = draw_queries(jax.random.fold_in(streams_of[7], 71), 0)
    key_rows = draw_key_rows(jax.random.fold_in(streams_of[7], 71), 0)
    value_rows = normal_values(streams_of[3], (ROLLOUTS, SEQ, HD), 1.0, 5.0, ((0, 8), (1, 4)))
    grad_output = normal_values(streams_of[4], (ROLLOUTS, SEQ, GROUP * HD), 2.0, 12.0, ((0, 8), (1, 4)))
    segments = jax.vmap(lambda own: jnp.searchsorted(jnp.cumsum(uneven_parts(own, DOCS, SEQ, SEQ // 2, 0)), jnp.arange(SEQ), side="right"))(jax.random.split(streams_of[5], ROLLOUTS)).reshape((ROLLOUTS, SEQ)).astype(jnp.int32)
    lengths = draw_lengths(jax.random.fold_in(streams_of[7], 71), 0)
    return dict(layer_input=layer_input, queries=queries, key_rows=key_rows, value_rows=value_rows, grad_output=grad_output, segments=segments, lengths=lengths)


def make_mask(query_seg, key_seg, query_pos, key_pos, length, window_len):
    gap = query_pos[:, None] - key_pos[None, :]
    same_doc = query_seg[:, None] == key_seg[None, :]
    inside = (gap >= 0) & (gap < window_len)
    alive = (key_pos[None, :] < length) | (gap == 0)
    return same_doc & inside & alive

def block_grads(query_blk, upstream, key_all, allowed, live, score_scale):
    head_size = key_all.shape[1] // 2
    key_part = key_all[:, :head_size].astype(jnp.float32)
    value_part = key_all[:, head_size:].astype(jnp.float32)
    query_f = query_blk.astype(jnp.float32)
    upstream_f = upstream.astype(jnp.float32)
    scores = jnp.einsum('rgd,kd->grk', query_f, key_part) * score_scale
    masked = jnp.where(allowed[None], scores, -1e+30)
    row_max = lax.optimization_barrier(jnp.max(masked, axis=2, keepdims=True))
    unnorm = jnp.where(allowed[None], jnp.exp(masked - row_max), 0.0)
    probs = unnorm / lax.optimization_barrier(jnp.sum(unnorm, axis=2, keepdims=True)) * live[None, :, None]
    probs_low = probs.astype(jnp.bfloat16).astype(jnp.float32)
    dprobs = jnp.einsum('rgd,kd->grk', upstream_f, value_part)
    row_dot = lax.optimization_barrier(jnp.sum(probs * dprobs, axis=2, keepdims=True))
    dscores = (probs * (dprobs - row_dot)).astype(jnp.bfloat16).astype(jnp.float32)
    grad_q = (jnp.einsum('grk,kd->rgd', dscores, key_part) * score_scale).astype(jnp.bfloat16)
    grad_k = jnp.einsum('grk,rgd->kd', dscores, query_f) * score_scale
    grad_v = jnp.einsum('grk,rgd->kd', probs_low, upstream_f)
    return (grad_q.reshape(query_blk.shape[0], -1), jnp.concatenate([grad_k, grad_v], axis=1))

def reference(layer_input, queries, key_rows, value_rows, grad_output, segments, lengths):
    window_len = WINDOW
    score_scale = 1.0 / math.sqrt(HD)

    def one_rollout(items):
        inputs_r, query_r, key_r, value_r, upstream_r, seg_r, length = items
        pair = jnp.concatenate([key_r, value_r], axis=1)
        pair_pad = jnp.concatenate([jnp.zeros((window_len, 2 * HD), jnp.bfloat16), pair], axis=0)
        seg_pad = jnp.concatenate([jnp.full((window_len,), -1, jnp.int32), seg_r.astype(jnp.int32)])

        def one_block(block):
            first_row = (block * ROWS).astype(jnp.int32)
            query_blk = lax.dynamic_slice_in_dim(query_r, first_row, ROWS, 0).reshape(ROWS, GROUP, HD)
            upstream = lax.dynamic_slice_in_dim(upstream_r, first_row, ROWS, 0).reshape(ROWS, GROUP, HD)
            key_all = lax.dynamic_slice_in_dim(pair_pad, first_row, window_len + ROWS, 0)
            query_seg = lax.dynamic_slice_in_dim(seg_r.astype(jnp.int32), first_row, ROWS, 0)
            key_seg = lax.dynamic_slice_in_dim(seg_pad, first_row, window_len + ROWS, 0)
            query_pos = first_row + jnp.arange(ROWS, dtype=jnp.int32)
            key_pos = first_row - window_len + jnp.arange(window_len + ROWS, dtype=jnp.int32)
            allowed = make_mask(query_seg, key_seg, query_pos, key_pos, length, window_len)
            live = (query_pos < length).astype(jnp.float32)
            return block_grads(query_blk, upstream, key_all, allowed, live, score_scale)
        grad_q, contrib = lax.map(one_block, jnp.arange(N_CTX, dtype=jnp.int32))
        contrib = contrib.reshape(N_CTX, SPAN + 1, ROWS, 2 * HD)
        total = jnp.zeros((N_CTX + SPAN, ROWS, 2 * HD), jnp.float32)
        for slot_index in range(SPAN + 1):
            total = total.at[slot_index:slot_index + N_CTX].add(contrib[:, slot_index])
        grad_kv = total[SPAN:].reshape(SEQ, 2 * HD).astype(jnp.bfloat16)
        rollout_grad = jnp.dot(inputs_r.T, grad_kv, preferred_element_type=jnp.float32)
        return (grad_q.reshape(SEQ, GROUP * HD), rollout_grad)
    grad_queries, rollout_grads = lax.map(one_rollout, (layer_input, queries, key_rows, value_rows, grad_output, segments, lengths))
    summed = lax.optimization_barrier(jnp.sum(rollout_grads, axis=0))
    grad_weights = (summed / N_DP).astype(jnp.bfloat16)
    return (grad_queries, grad_weights)
```

```python
import functools
import math

import jax
import jax.numpy as jnp
from jax import lax
from jax.experimental import pallas as pl
from jax.experimental.pallas import tpu as pltpu
from jax.sharding import PartitionSpec as P

F32 = jnp.float32
BF16 = jnp.bfloat16
LOG2E = 1.4426950408889634
NT = (((1,), (1,)), ((), ()))


def passed_along(x, axis, by):
    length = lax.axis_size(axis)
    pairs = [(i, i + by) for i in range(length) if 0 <= i + by < length]
    return lax.ppermute(x, axis, pairs)


def make_mask(query_seg, key_seg, query_pos, key_pos, length, window_len):
    gap = query_pos[:, None] - key_pos[None, :]
    same_doc = query_seg[:, None] == key_seg[None, :]
    inside = (gap >= 0) & (gap < window_len)
    alive = (key_pos[None, :] < length) | (gap == 0)
    return same_doc & inside & alive


def block_grads(query_blk, upstream, key_all, allowed, live, score_scale):
    head_size = key_all.shape[1] // 2
    key_part = key_all[:, :head_size]
    value_part = key_all[:, head_size:]
    scores = (
        jnp.einsum("rgd,kd->grk", query_blk, key_part, preferred_element_type=jnp.float32)
        * score_scale
    )
    masked = jnp.where(allowed[None], scores, -1e30)
    row_max = jnp.max(masked, axis=2, keepdims=True)
    unnorm = jnp.where(allowed[None], jnp.exp(masked - row_max), 0.0)
    probs = unnorm / jnp.sum(unnorm, axis=2, keepdims=True) * live[None, :, None]
    probs_low = probs.astype(jnp.bfloat16)
    dprobs = jnp.einsum("rgd,kd->grk", upstream, value_part, preferred_element_type=jnp.float32)
    row_dot = jnp.sum(probs * dprobs, axis=2, keepdims=True)
    dscores = (probs * (dprobs - row_dot)).astype(jnp.bfloat16)
    grad_q = (
        jnp.einsum("grk,kd->rgd", dscores, key_part, preferred_element_type=jnp.float32)
        * score_scale
    ).astype(jnp.bfloat16)
    grad_k = (
        jnp.einsum("grk,rgd->kd", dscores, query_blk, preferred_element_type=jnp.float32)
        * score_scale
    )
    grad_v = jnp.einsum("grk,rgd->kd", probs_low, upstream, preferred_element_type=jnp.float32)
    return (grad_q.reshape(query_blk.shape[0], -1), jnp.concatenate([grad_k, grad_v], axis=1))


def shards(layer_input, queries, key_rows, value_rows, grad_output, segments, lengths):
    ctx_count = lax.axis_size("ctx")
    dp_count = lax.axis_size("dp")
    ctx_place = lax.axis_index("ctx")
    row_count = layer_input.shape[1]
    width_all = layer_input.shape[2]
    head_size = key_rows.shape[2]
    group_size = queries.shape[2] // head_size
    reach_count = min(8, ctx_count // 2)
    window_len = reach_count * row_count
    score_scale = 1.0 / math.sqrt(head_size)
    local_pair = jnp.concatenate([key_rows[0], value_rows[0]], axis=1)
    earlier = []
    for offset in range(1, reach_count + 1):
        earlier.append(passed_along(local_pair, "ctx", offset))
    key_all = jnp.concatenate(earlier[::-1] + [local_pair], axis=0)
    length = lengths[0]
    seg_row = segments[0]
    seg_pad = jnp.concatenate([jnp.full((window_len,), -1, jnp.int32), seg_row])
    first_row = ctx_place * row_count
    query_seg = lax.dynamic_slice_in_dim(seg_row, first_row, row_count, 0)
    key_seg = lax.dynamic_slice_in_dim(seg_pad, first_row, window_len + row_count, 0)
    query_pos = first_row + jnp.arange(row_count, dtype=jnp.int32)
    key_pos = first_row - window_len + jnp.arange(window_len + row_count, dtype=jnp.int32)
    allowed = make_mask(query_seg, key_seg, query_pos, key_pos, length, window_len)
    live = (query_pos < length).astype(jnp.float32)
    query_blk = queries[0].reshape(row_count, group_size, head_size)
    upstream = grad_output[0].reshape(row_count, group_size, head_size)
    grad_q, contrib = block_grads(query_blk, upstream, key_all, allowed, live, score_scale)
    blocks = contrib.reshape(reach_count + 1, row_count, 2 * head_size)
    total = blocks[reach_count]
    for offset in range(1, reach_count + 1):
        total = total + passed_along(blocks[reach_count - offset], "ctx", -offset)
    grad_kv = total.astype(jnp.bfloat16)
    slab_rows = width_all // (dp_count * ctx_count)
    inputs_flat = layer_input[0]
    partial_value = jnp.einsum(
        "rd,rc->dc", inputs_flat, grad_kv, preferred_element_type=jnp.float32
    )
    pieces = partial_value.reshape(dp_count, ctx_count, slab_rows, 2 * head_size)
    moved = lax.all_to_all(pieces, "ctx", split_axis=1, concat_axis=1, tiled=True)
    rollout_part = jnp.sum(moved, axis=1).reshape(dp_count * slab_rows, 2 * head_size)
    summed = lax.psum_scatter(rollout_part, "dp", scatter_dimension=0, tiled=True)
    grad_weights = (summed / dp_count).astype(jnp.bfloat16)
    return (grad_q.reshape(1, row_count, group_size * head_size), grad_weights)


def fused_kernel(
    n_dp, n_ctx, reach,
    x_ref, q_ref, k_ref, v_ref, go_ref, seg_ref, len_ref,
    gq_ref, gw_ref,
    kbuf, vbuf, qs, gos, bias, p_low, ds_low, gsend, grecv, gkv_t, xbuf, csend, crecv, zsend, zrecv,
    load_sem, xl_sem, kv_ss, kv_rs, g_ss, g_rs, a_ss, a_rs, x_ss, x_rs, c_ss, c_rs, z_ss, z_rs,
):
    rows = k_ref.shape[0]
    head = k_ref.shape[1]
    group = q_ref.shape[1] // head
    slab = gw_ref.shape[0]
    nz = n_dp // 2
    window = reach * rows
    scale = 1.0 / math.sqrt(head)
    dp = lax.axis_index("dp")
    ctx = lax.axis_index("ctx")
    z = dp // 2
    core = dp % 2
    sibling = z * 2 + (1 - core)

    def remote(src, dst, ss, rs, dp_to, ctx_to):
        return pltpu.make_async_remote_copy(
            src_ref=src, dst_ref=dst, send_sem=ss, recv_sem=rs,
            device_id={"dp": dp_to, "ctx": ctx_to}, device_id_type=pl.DeviceIdType.MESH,
        )

    loads = []
    for h in range(group):
        cols = pl.ds(h * head, head)
        loads.append(pltpu.make_async_copy(q_ref.at[:, cols], qs.at[pl.ds(h * rows, rows)], load_sem.at[2 * h]))
        loads.append(pltpu.make_async_copy(go_ref.at[:, cols], gos.at[pl.ds(h * rows, rows)], load_sem.at[2 * h + 1]))
    loads.append(pltpu.make_async_copy(k_ref, kbuf.at[pl.ds(window, rows)], load_sem.at[2 * group]))
    loads.append(pltpu.make_async_copy(v_ref, vbuf.at[pl.ds(window, rows)], load_sem.at[2 * group + 1]))
    for copy in loads:
        copy.start()

    barrier = pltpu.get_barrier_semaphore()
    for o in range(1, n_ctx):
        pl.semaphore_signal(barrier, inc=1, device_id={"dp": dp, "ctx": (ctx + o) % n_ctx}, device_id_type=pl.DeviceIdType.MESH)
    pl.semaphore_signal(barrier, inc=1, device_id={"dp": sibling, "ctx": ctx}, device_id_type=pl.DeviceIdType.MESH)
    for o in range(1, nz):
        pl.semaphore_signal(barrier, inc=1, device_id={"dp": ((z + o) % nz) * 2 + core, "ctx": ctx}, device_id_type=pl.DeviceIdType.MESH)
    pl.semaphore_wait(barrier, n_ctx - 1 + 1 + nz - 1)

    def kv_copies(off, to):
        slot = pl.ds((reach - off) * rows, rows)
        return (
            remote(k_ref, kbuf.at[slot], kv_ss.at[off - 1, 0], kv_rs.at[off - 1, 0], dp, to),
            remote(v_ref, vbuf.at[slot], kv_ss.at[off - 1, 1], kv_rs.at[off - 1, 1], dp, to),
        )

    for off in range(1, reach + 1):
        @pl.when(ctx + off < n_ctx)
        def _():
            for copy in kv_copies(off, (ctx + off) % n_ctx):
                copy.start()

    def piece_dp(k, s):
        return ((z + 1 + k) % nz) * 2 + (1 - core if s == 0 else core)

    def x_copy(k, s, o, source, to):
        d = piece_dp(k, s)
        cols = pl.ds(pl.multiple_of((d * n_ctx + to) * slab, slab), slab)
        return remote(
            x_ref.at[:, cols], xbuf.at[d, pl.ds(pl.multiple_of(source * rows, rows), rows)],
            x_ss.at[k, s, o - 1], x_rs.at[k, s, o - 1], dp, to,
        )

    def x_local(k, s):
        d = piece_dp(k, s)
        cols = pl.ds(pl.multiple_of((d * n_ctx + ctx) * slab, slab), slab)
        return pltpu.make_async_copy(
            x_ref.at[:, cols], xbuf.at[d, pl.ds(pl.multiple_of(ctx * rows, rows), rows)], xl_sem.at[k, s]
        )

    for k in range(nz):
        for s in range(2):
            for o in range(1, n_ctx):
                x_copy(k, s, o, ctx, (ctx + o) % n_ctx).start()
            x_local(k, s).start()

    length = len_ref[0]
    key_at = lax.broadcasted_iota(jnp.int32, (rows, rows), 0)
    query_at = lax.broadcasted_iota(jnp.int32, (rows, rows), 1) + ctx * rows
    query_seg = seg_ref[:, pl.ds(pl.multiple_of(ctx * rows, rows), rows)].astype(F32)
    for b in range(reach + 1):
        first = (ctx - (reach - b)) * rows
        from_row = pl.multiple_of(jnp.maximum(ctx - (reach - b), 0) * rows, rows)
        key_seg = jnp.broadcast_to(seg_ref[:, pl.ds(from_row, rows)].astype(F32), (rows, rows)).T
        key_pos = key_at + first
        gap = query_at - key_pos
        ok = (key_seg == query_seg) & (gap >= 0) & (gap < window) & (key_pos >= 0)
        ok = ok & ((key_pos < length) | (gap == 0))
        bias[pl.ds(b * rows, rows), :] = jnp.where(ok, 0.0, -1e30)
    live = (lax.broadcasted_iota(jnp.int32, (1, rows), 1) + ctx * rows < length).astype(F32)

    for off in range(1, reach + 1):
        slot = pl.ds((reach - off) * rows, rows)

        @pl.when(ctx - off < 0)
        def _():
            kbuf[slot, :] = jnp.zeros((rows, head), BF16)
            vbuf[slot, :] = jnp.zeros((rows, head), BF16)

    for copy in loads:
        copy.wait()
    for off in range(1, reach + 1):
        @pl.when(ctx - off >= 0)
        def _():
            for copy in kv_copies(off, ctx):
                copy.wait_recv()

    for h in range(group):
        here = pl.ds(h * rows, rows)
        score = lax.dot_general(kbuf[...], qs[here, :], NT, preferred_element_type=F32) + bias[...]
        top = jnp.max(score, axis=0, keepdims=True)
        unnorm = jnp.exp2((score - top) * (scale * LOG2E))
        probs = unnorm * (live / jnp.sum(unnorm, axis=0, keepdims=True))
        p_low[:, here] = probs.astype(BF16)
        dprobs = lax.dot_general(vbuf[...], gos[here, :], NT, preferred_element_type=F32)
        row_dot = jnp.sum(probs * dprobs, axis=0, keepdims=True)
        ds_low[:, here] = (probs * (dprobs - row_dot)).astype(BF16)

    def kv_grad(b):
        block = pl.ds(b * rows, rows)
        gk = jnp.dot(ds_low[block, :], qs[...], preferred_element_type=F32) * scale
        gv = jnp.dot(p_low[block, :], gos[...], preferred_element_type=F32)
        return gk, gv

    def g_copy(off, to):
        return remote(gsend.at[off - 1], grecv.at[off - 1], g_ss.at[off - 1], g_rs.at[off - 1], dp, to)

    for off in range(1, reach + 1):
        gk, gv = kv_grad(reach - off)
        gsend[off - 1, :, pl.ds(0, head)] = gk.astype(BF16)
        gsend[off - 1, :, pl.ds(head, head)] = gv.astype(BF16)

        @pl.when(ctx - off >= 0)
        def _():
            g_copy(off, (ctx + n_ctx - off) % n_ctx).start()

        @pl.when(ctx + off >= n_ctx)
        def _():
            grecv[off - 1] = jnp.zeros((rows, 2 * head), BF16)

    gk, gv = kv_grad(reach)

    key_t = kbuf[...].astype(F32).T.astype(BF16)
    for h in range(group):
        here = pl.ds(h * rows, rows)
        gq_t = jnp.dot(key_t, ds_low[:, here], preferred_element_type=F32) * scale
        gq_ref[:, pl.ds(h * head, head)] = gq_t.T.astype(BF16)

    for off in range(1, reach + 1):
        @pl.when(ctx + off < n_ctx)
        def _():
            g_copy(off, ctx).wait_recv()
    for off in range(1, reach + 1):
        gk = gk + grecv[off - 1, :, pl.ds(0, head)].astype(F32)
        gv = gv + grecv[off - 1, :, pl.ds(head, head)].astype(F32)
    own = pl.ds(pl.multiple_of(ctx * rows, rows), rows)
    gkv_t[pl.ds(0, head), own] = gk.T.astype(BF16)
    gkv_t[pl.ds(head, head), own] = gv.T.astype(BF16)

    def a_copy(o, source, to):
        part = gkv_t.at[:, pl.ds(pl.multiple_of(source * rows, rows), rows)]
        return remote(part, part, a_ss.at[o - 1], a_rs.at[o - 1], dp, to)

    for o in range(1, n_ctx):
        a_copy(o, ctx, (ctx + o) % n_ctx).start()
    for o in range(1, n_ctx):
        a_copy(o, (ctx + n_ctx - o) % n_ctx, ctx).wait_recv()

    def product(k, s):
        for o in range(1, n_ctx):
            x_copy(k, s, o, (ctx + n_ctx - o) % n_ctx, ctx).wait_recv()
        x_local(k, s).wait()
        return jnp.dot(gkv_t[...], xbuf[piece_dp(k, s)], preferred_element_type=F32)

    def c_copy(k):
        return remote(csend.at[k], crecv.at[k], c_ss.at[k], c_rs.at[k], sibling, ctx)

    def z_copy(k):
        return remote(zsend.at[k], zrecv.at[k], z_ss.at[k], z_rs.at[k], piece_dp(k, 1), ctx)

    total = None
    for k in range(nz):
        csend[k] = product(k, 0).astype(BF16)
        c_copy(k).start()
        part = product(k, 1)
        c_copy(k).wait_recv()
        part = part + crecv[k].astype(F32)
        if k < nz - 1:
            zsend[k] = part.astype(BF16)
            z_copy(k).start()
        else:
            total = part
    for k in range(nz - 1):
        z_copy(k).wait_recv()
        total = total + zrecv[k].astype(F32)
    gw_ref[...] = (total * (1.0 / n_dp)).T.astype(BF16)

    for off in range(1, reach + 1):
        @pl.when(ctx + off < n_ctx)
        def _():
            for copy in kv_copies(off, (ctx + off) % n_ctx):
                copy.wait_send()

        @pl.when(ctx - off >= 0)
        def _():
            g_copy(off, (ctx + n_ctx - off) % n_ctx).wait_send()
    for o in range(1, n_ctx):
        a_copy(o, ctx, (ctx + o) % n_ctx).wait_send()
    for k in range(nz):
        for s in range(2):
            for o in range(1, n_ctx):
                x_copy(k, s, o, ctx, (ctx + o) % n_ctx).wait_send()
        c_copy(k).wait_send()
        if k < nz - 1:
            z_copy(k).wait_send()


def fused_shards(layer_input, queries, key_rows, value_rows, grad_output, segments, lengths):
    n_dp = lax.axis_size("dp")
    n_ctx = lax.axis_size("ctx")
    rows, width = layer_input.shape[1:]
    head = key_rows.shape[2]
    group = queries.shape[2] // head
    reach = min(8, n_ctx // 2)
    keys = (reach + 1) * rows
    slab = width // (n_dp * n_ctx)
    nz = n_dp // 2
    dma = pltpu.SemaphoreType.DMA
    anywhere = pl.BlockSpec(memory_space=pl.ANY)
    vmem = pl.BlockSpec(memory_space=pltpu.VMEM)
    smem = pl.BlockSpec(memory_space=pltpu.SMEM)
    gq, gw = pl.pallas_call(
        functools.partial(fused_kernel, n_dp, n_ctx, reach),
        out_shape=(
            jax.ShapeDtypeStruct((rows, group * head), BF16),
            jax.ShapeDtypeStruct((slab, 2 * head), BF16),
        ),
        in_specs=[anywhere] * 5 + [vmem, smem],
        out_specs=(vmem, vmem),
        scratch_shapes=[
            pltpu.VMEM((keys, head), BF16),
            pltpu.VMEM((keys, head), BF16),
            pltpu.VMEM((group * rows, head), BF16),
            pltpu.VMEM((group * rows, head), BF16),
            pltpu.VMEM((keys, rows), F32),
            pltpu.VMEM((keys, group * rows), BF16),
            pltpu.VMEM((keys, group * rows), BF16),
            pltpu.VMEM((reach, rows, 2 * head), BF16),
            pltpu.VMEM((reach, rows, 2 * head), BF16),
            pltpu.VMEM((2 * head, n_ctx * rows), BF16),
            pltpu.VMEM((n_dp, n_ctx * rows, slab), BF16),
            pltpu.VMEM((nz, 2 * head, slab), BF16),
            pltpu.VMEM((nz, 2 * head, slab), BF16),
            pltpu.VMEM((nz - 1, 2 * head, slab), BF16),
            pltpu.VMEM((nz - 1, 2 * head, slab), BF16),
            dma((2 * group + 2,)),
            dma((nz, 2)),
            dma((reach, 2)),
            dma((reach, 2)),
            dma((reach,)),
            dma((reach,)),
            dma((n_ctx - 1,)),
            dma((n_ctx - 1,)),
            dma((nz, 2, n_ctx - 1)),
            dma((nz, 2, n_ctx - 1)),
            dma((nz,)),
            dma((nz,)),
            dma((nz - 1,)),
            dma((nz - 1,)),
        ],
        compiler_params=pltpu.CompilerParams(
            collective_id=0, has_side_effects=True, vmem_limit_bytes=40 * 1024 * 1024
        ),
    )(layer_input[0], queries[0], key_rows[0], value_rows[0], grad_output[0], segments, lengths)
    return gq[None], gw


def by_size(layer_input, *rest):
    n_dp, n_ctx = lax.axis_size("dp"), lax.axis_size("ctx")
    slab = layer_input.shape[2] // (n_dp * n_ctx)
    whole_tiles = slab % 128 == 0 and layer_input.shape[1] % 128 == 0
    run = fused_shards if whole_tiles and n_dp % 2 == 0 and n_dp > 2 else shards
    return run(layer_input, *rest)


def solution(mesh):
    return jax.shard_map(
        by_size,
        mesh=mesh,
        in_specs=(
            P("dp", "ctx", None),
            P("dp", "ctx", None),
            P("dp", "ctx", None),
            P("dp", "ctx", None),
            P("dp", "ctx", None),
            P("dp", None),
            P("dp"),
        ),
        out_specs=(P("dp", "ctx", None), P(("dp", "ctx"), None)),
        check_vma=False,
    )
```

```python
import functools
import math

import jax
import jax.numpy as jnp
from jax import lax
from jax.experimental import pallas as pl
from jax.experimental.pallas import tpu as pltpu
from jax.sharding import PartitionSpec as P

F32 = jnp.float32
BF16 = jnp.bfloat16
LOG2E = 1.4426950408889634
NT = (((1,), (1,)), ((), ()))


def passed_along(x, axis, by):
    length = lax.axis_size(axis)
    pairs = [(i, i + by) for i in range(length) if 0 <= i + by < length]
    return lax.ppermute(x, axis, pairs)


def make_mask(query_seg, key_seg, query_pos, key_pos, length, window_len):
    gap = query_pos[:, None] - key_pos[None, :]
    same_doc = query_seg[:, None] == key_seg[None, :]
    inside = (gap >= 0) & (gap < window_len)
    alive = (key_pos[None, :] < length) | (gap == 0)
    return same_doc & inside & alive


def block_grads(query_blk, upstream, key_all, allowed, live, score_scale):
    head_size = key_all.shape[1] // 2
    key_part = key_all[:, :head_size]
    value_part = key_all[:, head_size:]
    scores = (
        jnp.einsum("rgd,kd->grk", query_blk, key_part, preferred_element_type=jnp.float32)
        * score_scale
    )
    masked = jnp.where(allowed[None], scores, -1e30)
    row_max = jnp.max(masked, axis=2, keepdims=True)
    unnorm = jnp.where(allowed[None], jnp.exp(masked - row_max), 0.0)
    probs = unnorm / jnp.sum(unnorm, axis=2, keepdims=True) * live[None, :, None]
    probs_low = probs.astype(jnp.bfloat16)
    dprobs = jnp.einsum("rgd,kd->grk", upstream, value_part, preferred_element_type=jnp.float32)
    row_dot = jnp.sum(probs * dprobs, axis=2, keepdims=True)
    dscores = (probs * (dprobs - row_dot)).astype(jnp.bfloat16)
    grad_q = (
        jnp.einsum("grk,kd->rgd", dscores, key_part, preferred_element_type=jnp.float32)
        * score_scale
    ).astype(jnp.bfloat16)
    grad_k = (
        jnp.einsum("grk,rgd->kd", dscores, query_blk, preferred_element_type=jnp.float32)
        * score_scale
    )
    grad_v = jnp.einsum("grk,rgd->kd", probs_low, upstream, preferred_element_type=jnp.float32)
    return (grad_q.reshape(query_blk.shape[0], -1), jnp.concatenate([grad_k, grad_v], axis=1))


def shards(layer_input, queries, key_rows, value_rows, grad_output, segments, lengths):
    ctx_count = lax.axis_size("ctx")
    dp_count = lax.axis_size("dp")
    ctx_place = lax.axis_index("ctx")
    row_count = layer_input.shape[1]
    width_all = layer_input.shape[2]
    head_size = key_rows.shape[2]
    group_size = queries.shape[2] // head_size
    reach_count = min(8, ctx_count // 2)
    window_len = reach_count * row_count
    score_scale = 1.0 / math.sqrt(head_size)
    local_pair = jnp.concatenate([key_rows[0], value_rows[0]], axis=1)
    earlier = []
    for offset in range(1, reach_count + 1):
        earlier.append(passed_along(local_pair, "ctx", offset))
    key_all = jnp.concatenate(earlier[::-1] + [local_pair], axis=0)
    length = lengths[0]
    seg_row = segments[0]
    seg_pad = jnp.concatenate([jnp.full((window_len,), -1, jnp.int32), seg_row])
    first_row = ctx_place * row_count
    query_seg = lax.dynamic_slice_in_dim(seg_row, first_row, row_count, 0)
    key_seg = lax.dynamic_slice_in_dim(seg_pad, first_row, window_len + row_count, 0)
    query_pos = first_row + jnp.arange(row_count, dtype=jnp.int32)
    key_pos = first_row - window_len + jnp.arange(window_len + row_count, dtype=jnp.int32)
    allowed = make_mask(query_seg, key_seg, query_pos, key_pos, length, window_len)
    live = (query_pos < length).astype(jnp.float32)
    query_blk = queries[0].reshape(row_count, group_size, head_size)
    upstream = grad_output[0].reshape(row_count, group_size, head_size)
    grad_q, contrib = block_grads(query_blk, upstream, key_all, allowed, live, score_scale)
    blocks = contrib.reshape(reach_count + 1, row_count, 2 * head_size)
    total = blocks[reach_count]
    for offset in range(1, reach_count + 1):
        total = total + passed_along(blocks[reach_count - offset], "ctx", -offset)
    grad_kv = total.astype(jnp.bfloat16)
    slab_rows = width_all // (dp_count * ctx_count)
    inputs_flat = layer_input[0]
    partial_value = jnp.einsum(
        "rd,rc->dc", inputs_flat, grad_kv, preferred_element_type=jnp.float32
    )
    pieces = partial_value.reshape(dp_count, ctx_count, slab_rows, 2 * head_size)
    moved = lax.all_to_all(pieces, "ctx", split_axis=1, concat_axis=1, tiled=True)
    rollout_part = jnp.sum(moved, axis=1).reshape(dp_count * slab_rows, 2 * head_size)
    summed = lax.psum_scatter(rollout_part, "dp", scatter_dimension=0, tiled=True)
    grad_weights = (summed / dp_count).astype(jnp.bfloat16)
    return (grad_q.reshape(1, row_count, group_size * head_size), grad_weights)


def fused_kernel(
    n_dp, n_ctx, reach,
    x_ref, q_ref, k_ref, v_ref, go_ref, seg_ref, len_ref,
    gq_ref, gw_ref,
    kbuf, vbuf, qs, gos, bias, p_low, ds_low, gsend, grecv, gkv_t, xbuf, csend, crecv, zsend, zrecv,
    load_sem, xl_sem, kv_ss, kv_rs, g_ss, g_rs, a_ss, a_rs, x_ss, x_rs, c_ss, c_rs, z_ss, z_rs,
):
    rows = k_ref.shape[0]
    head = k_ref.shape[1]
    group = q_ref.shape[1] // head
    slab = gw_ref.shape[0]
    nz = n_dp // 2
    window = reach * rows
    scale = 1.0 / math.sqrt(head)
    dp = lax.axis_index("dp")
    ctx = lax.axis_index("ctx")
    z = dp // 2
    core = dp % 2
    sibling = z * 2 + (1 - core)

    def remote(src, dst, ss, rs, dp_to, ctx_to):
        return pltpu.make_async_remote_copy(
            src_ref=src, dst_ref=dst, send_sem=ss, recv_sem=rs,
            device_id={"dp": dp_to, "ctx": ctx_to}, device_id_type=pl.DeviceIdType.MESH,
        )

    loads = []
    for h in range(group):
        cols = pl.ds(h * head, head)
        loads.append(pltpu.make_async_copy(q_ref.at[:, cols], qs.at[pl.ds(h * rows, rows)], load_sem.at[2 * h]))
        loads.append(pltpu.make_async_copy(go_ref.at[:, cols], gos.at[pl.ds(h * rows, rows)], load_sem.at[2 * h + 1]))
    loads.append(pltpu.make_async_copy(k_ref, kbuf.at[pl.ds(window, rows)], load_sem.at[2 * group]))
    loads.append(pltpu.make_async_copy(v_ref, vbuf.at[pl.ds(window, rows)], load_sem.at[2 * group + 1]))
    for copy in loads:
        copy.start()

    barrier = pltpu.get_barrier_semaphore()
    for o in range(1, n_ctx):
        pl.semaphore_signal(barrier, inc=1, device_id={"dp": dp, "ctx": (ctx + o) % n_ctx}, device_id_type=pl.DeviceIdType.MESH)
    pl.semaphore_signal(barrier, inc=1, device_id={"dp": sibling, "ctx": ctx}, device_id_type=pl.DeviceIdType.MESH)
    for o in range(1, nz):
        pl.semaphore_signal(barrier, inc=1, device_id={"dp": ((z + o) % nz) * 2 + core, "ctx": ctx}, device_id_type=pl.DeviceIdType.MESH)
    pl.semaphore_wait(barrier, n_ctx - 1 + 1 + nz - 1)

    def kv_copies(off, to):
        slot = pl.ds((reach - off) * rows, rows)
        return (
            remote(k_ref, kbuf.at[slot], kv_ss.at[off - 1, 0], kv_rs.at[off - 1, 0], dp, to),
            remote(v_ref, vbuf.at[slot], kv_ss.at[off - 1, 1], kv_rs.at[off - 1, 1], dp, to),
        )

    for off in range(1, reach + 1):
        @pl.when(ctx + off < n_ctx)
        def _():
            for copy in kv_copies(off, (ctx + off) % n_ctx):
                copy.start()

    def piece_dp(k, s):
        return ((z + 1 + k) % nz) * 2 + (1 - core if s == 0 else core)

    def x_copy(k, s, o, source, to):
        d = piece_dp(k, s)
        cols = pl.ds(pl.multiple_of((d * n_ctx + to) * slab, slab), slab)
        return remote(
            x_ref.at[:, cols], xbuf.at[d, pl.ds(pl.multiple_of(source * rows, rows), rows)],
            x_ss.at[k, s, o - 1], x_rs.at[k, s, o - 1], dp, to,
        )

    def x_local(k, s):
        d = piece_dp(k, s)
        cols = pl.ds(pl.multiple_of((d * n_ctx + ctx) * slab, slab), slab)
        return pltpu.make_async_copy(
            x_ref.at[:, cols], xbuf.at[d, pl.ds(pl.multiple_of(ctx * rows, rows), rows)], xl_sem.at[k, s]
        )

    pieces = [(k, s) for k in range(nz) for s in range(2)]

    def issue(some):
        for k, s in some:
            for o in range(1, n_ctx):
                x_copy(k, s, o, ctx, (ctx + o) % n_ctx).start()
            x_local(k, s).start()

    issue(pieces[:2])

    length = len_ref[0]
    key_at = lax.broadcasted_iota(jnp.int32, (rows, rows), 0)
    query_at = lax.broadcasted_iota(jnp.int32, (rows, rows), 1) + ctx * rows
    query_seg = seg_ref[:, pl.ds(pl.multiple_of(ctx * rows, rows), rows)].astype(F32)
    for b in range(reach + 1):
        first = (ctx - (reach - b)) * rows
        from_row = pl.multiple_of(jnp.maximum(ctx - (reach - b), 0) * rows, rows)
        key_seg = jnp.broadcast_to(seg_ref[:, pl.ds(from_row, rows)].astype(F32), (rows, rows)).T
        key_pos = key_at + first
        gap = query_at - key_pos
        ok = (key_seg == query_seg) & (gap >= 0) & (gap < window) & (key_pos >= 0)
        ok = ok & ((key_pos < length) | (gap == 0))
        bias[pl.ds(b * rows, rows), :] = jnp.where(ok, 0.0, -1e30)
    live = (lax.broadcasted_iota(jnp.int32, (1, rows), 1) + ctx * rows < length).astype(F32)

    for off in range(1, reach + 1):
        slot = pl.ds((reach - off) * rows, rows)

        @pl.when(ctx - off < 0)
        def _():
            kbuf[slot, :] = jnp.zeros((rows, head), BF16)
            vbuf[slot, :] = jnp.zeros((rows, head), BF16)

    for copy in loads:
        copy.wait()
    for off in range(1, reach + 1):
        @pl.when(ctx - off >= 0)
        def _():
            for copy in kv_copies(off, ctx):
                copy.wait_recv()

    for h in range(group):
        if h == group // 2:
            issue(pieces[2:3])
        here = pl.ds(h * rows, rows)
        score = lax.dot_general(kbuf[...], qs[here, :], NT, preferred_element_type=F32) + bias[...]
        top = jnp.max(score, axis=0, keepdims=True)
        unnorm = jnp.exp2((score - top) * (scale * LOG2E))
        probs = unnorm * (live / jnp.sum(unnorm, axis=0, keepdims=True))
        p_low[:, here] = probs.astype(BF16)
        dprobs = lax.dot_general(vbuf[...], gos[here, :], NT, preferred_element_type=F32)
        row_dot = jnp.sum(probs * dprobs, axis=0, keepdims=True)
        ds_low[:, here] = (probs * (dprobs - row_dot)).astype(BF16)

    def kv_grad(b):
        block = pl.ds(b * rows, rows)
        gk = jnp.dot(ds_low[block, :], qs[...], preferred_element_type=F32) * scale
        gv = jnp.dot(p_low[block, :], gos[...], preferred_element_type=F32)
        return gk, gv

    def g_copy(off, to):
        return remote(gsend.at[off - 1], grecv.at[off - 1], g_ss.at[off - 1], g_rs.at[off - 1], dp, to)

    for off in range(1, reach + 1):
        gk, gv = kv_grad(reach - off)
        gsend[off - 1, :, pl.ds(0, head)] = gk.astype(BF16)
        gsend[off - 1, :, pl.ds(head, head)] = gv.astype(BF16)

        @pl.when(ctx - off >= 0)
        def _():
            g_copy(off, (ctx + n_ctx - off) % n_ctx).start()

        @pl.when(ctx + off >= n_ctx)
        def _():
            grecv[off - 1] = jnp.zeros((rows, 2 * head), BF16)

    issue(pieces[3:4])
    gk, gv = kv_grad(reach)

    key_t = kbuf[...].astype(F32).T.astype(BF16)
    for h in range(group):
        here = pl.ds(h * rows, rows)
        gq_t = jnp.dot(key_t, ds_low[:, here], preferred_element_type=F32) * scale
        gq_ref[:, pl.ds(h * head, head)] = gq_t.T.astype(BF16)

    for off in range(1, reach + 1):
        @pl.when(ctx + off < n_ctx)
        def _():
            g_copy(off, ctx).wait_recv()
    for off in range(1, reach + 1):
        gk = gk + grecv[off - 1, :, pl.ds(0, head)].astype(F32)
        gv = gv + grecv[off - 1, :, pl.ds(head, head)].astype(F32)
    own = pl.ds(pl.multiple_of(ctx * rows, rows), rows)
    gkv_t[pl.ds(0, head), own] = gk.T.astype(BF16)
    gkv_t[pl.ds(head, head), own] = gv.T.astype(BF16)

    def a_copy(o, source, to):
        part = gkv_t.at[:, pl.ds(pl.multiple_of(source * rows, rows), rows)]
        return remote(part, part, a_ss.at[o - 1], a_rs.at[o - 1], dp, to)

    for o in range(1, n_ctx):
        a_copy(o, ctx, (ctx + o) % n_ctx).start()
    issue(pieces[4:])
    for o in range(1, n_ctx):
        a_copy(o, (ctx + n_ctx - o) % n_ctx, ctx).wait_recv()

    def product(k, s):
        for o in range(1, n_ctx):
            x_copy(k, s, o, (ctx + n_ctx - o) % n_ctx, ctx).wait_recv()
        x_local(k, s).wait()
        return jnp.dot(gkv_t[...], xbuf[piece_dp(k, s)], preferred_element_type=F32)

    def c_copy(k):
        return remote(csend.at[k], crecv.at[k], c_ss.at[k], c_rs.at[k], sibling, ctx)

    def z_copy(k):
        return remote(zsend.at[k], zrecv.at[k], z_ss.at[k], z_rs.at[k], piece_dp(k, 1), ctx)

    def to_sibling(k):
        csend[k] = product(k, 0).astype(BF16)
        c_copy(k).start()

    total = None
    to_sibling(0)
    for k in range(nz):
        if k == 0:
            to_sibling(1)
        elif k > 1:
            to_sibling(k)
        part = product(k, 1)
        c_copy(k).wait_recv()
        part = part + crecv[k].astype(F32)
        if k < nz - 1:
            zsend[k] = part.astype(BF16)
            z_copy(k).start()
        else:
            total = part
    for k in range(nz - 1):
        z_copy(k).wait_recv()
        total = total + zrecv[k].astype(F32)
    gw_ref[...] = (total * (1.0 / n_dp)).T.astype(BF16)

    for off in range(1, reach + 1):
        @pl.when(ctx + off < n_ctx)
        def _():
            for copy in kv_copies(off, (ctx + off) % n_ctx):
                copy.wait_send()

        @pl.when(ctx - off >= 0)
        def _():
            g_copy(off, (ctx + n_ctx - off) % n_ctx).wait_send()
    for o in range(1, n_ctx):
        a_copy(o, ctx, (ctx + o) % n_ctx).wait_send()
    for k in range(nz):
        for s in range(2):
            for o in range(1, n_ctx):
                x_copy(k, s, o, ctx, (ctx + o) % n_ctx).wait_send()
        c_copy(k).wait_send()
        if k < nz - 1:
            z_copy(k).wait_send()


def fused_shards(layer_input, queries, key_rows, value_rows, grad_output, segments, lengths):
    n_dp = lax.axis_size("dp")
    n_ctx = lax.axis_size("ctx")
    rows, width = layer_input.shape[1:]
    head = key_rows.shape[2]
    group = queries.shape[2] // head
    reach = min(8, n_ctx // 2)
    keys = (reach + 1) * rows
    slab = width // (n_dp * n_ctx)
    nz = n_dp // 2
    dma = pltpu.SemaphoreType.DMA
    hbm = pl.BlockSpec(memory_space=pltpu.HBM)
    vmem = pl.BlockSpec(memory_space=pltpu.VMEM)
    smem = pl.BlockSpec(memory_space=pltpu.SMEM)
    gq, gw = pl.pallas_call(
        functools.partial(fused_kernel, n_dp, n_ctx, reach),
        out_shape=(
            jax.ShapeDtypeStruct((rows, group * head), BF16),
            jax.ShapeDtypeStruct((slab, 2 * head), BF16),
        ),
        in_specs=[hbm] * 5 + [vmem, smem],
        out_specs=(vmem, vmem),
        scratch_shapes=[
            pltpu.VMEM((keys, head), BF16),
            pltpu.VMEM((keys, head), BF16),
            pltpu.VMEM((group * rows, head), BF16),
            pltpu.VMEM((group * rows, head), BF16),
            pltpu.VMEM((keys, rows), F32),
            pltpu.VMEM((keys, group * rows), BF16),
            pltpu.VMEM((keys, group * rows), BF16),
            pltpu.VMEM((reach, rows, 2 * head), BF16),
            pltpu.VMEM((reach, rows, 2 * head), BF16),
            pltpu.VMEM((2 * head, n_ctx * rows), BF16),
            pltpu.VMEM((n_dp, n_ctx * rows, slab), BF16),
            pltpu.VMEM((nz, 2 * head, slab), BF16),
            pltpu.VMEM((nz, 2 * head, slab), BF16),
            pltpu.VMEM((nz - 1, 2 * head, slab), BF16),
            pltpu.VMEM((nz - 1, 2 * head, slab), BF16),
            dma((2 * group + 2,)),
            dma((nz, 2)),
            dma((reach, 2)),
            dma((reach, 2)),
            dma((reach,)),
            dma((reach,)),
            dma((n_ctx - 1,)),
            dma((n_ctx - 1,)),
            dma((nz, 2, n_ctx - 1)),
            dma((nz, 2, n_ctx - 1)),
            dma((nz,)),
            dma((nz,)),
            dma((nz - 1,)),
            dma((nz - 1,)),
        ],
        compiler_params=pltpu.CompilerParams(
            collective_id=0, has_side_effects=True, vmem_limit_bytes=40 * 1024 * 1024
        ),
    )(layer_input[0], queries[0], key_rows[0], value_rows[0], grad_output[0], segments, lengths)
    return gq[None], gw


def by_size(layer_input, *rest):
    n_dp, n_ctx = lax.axis_size("dp"), lax.axis_size("ctx")
    slab = layer_input.shape[2] // (n_dp * n_ctx)
    whole_tiles = slab % 128 == 0 and layer_input.shape[1] % 128 == 0
    run = fused_shards if whole_tiles and n_dp % 2 == 0 and n_dp > 2 else shards
    return run(layer_input, *rest)


def solution(mesh):
    return jax.shard_map(
        by_size,
        mesh=mesh,
        in_specs=(
            P("dp", "ctx", None),
            P("dp", "ctx", None),
            P("dp", "ctx", None),
            P("dp", "ctx", None),
            P("dp", "ctx", None),
            P("dp", None),
            P("dp"),
        ),
        out_specs=(P("dp", "ctx", None), P(("dp", "ctx"), None)),
        check_vma=False,
    )
```

```python
import functools
import math

import jax
import jax.numpy as jnp
from jax import lax
from jax.experimental import pallas as pl
from jax.experimental.pallas import tpu as pltpu
from jax.sharding import PartitionSpec as P

F32 = jnp.float32
BF16 = jnp.bfloat16
LOG2E = 1.4426950408889634
NT = (((1,), (1,)), ((), ()))


def passed_along(x, axis, by):
    length = lax.axis_size(axis)
    pairs = [(i, i + by) for i in range(length) if 0 <= i + by < length]
    return lax.ppermute(x, axis, pairs)


def make_mask(query_seg, key_seg, query_pos, key_pos, length, window_len):
    gap = query_pos[:, None] - key_pos[None, :]
    same_doc = query_seg[:, None] == key_seg[None, :]
    inside = (gap >= 0) & (gap < window_len)
    alive = (key_pos[None, :] < length) | (gap == 0)
    return same_doc & inside & alive


def block_grads(query_blk, upstream, key_all, allowed, live, score_scale):
    head_size = key_all.shape[1] // 2
    key_part = key_all[:, :head_size]
    value_part = key_all[:, head_size:]
    scores = (
        jnp.einsum("rgd,kd->grk", query_blk, key_part, preferred_element_type=jnp.float32)
        * score_scale
    )
    masked = jnp.where(allowed[None], scores, -1e30)
    row_max = jnp.max(masked, axis=2, keepdims=True)
    unnorm = jnp.where(allowed[None], jnp.exp(masked - row_max), 0.0)
    probs = unnorm / jnp.sum(unnorm, axis=2, keepdims=True) * live[None, :, None]
    probs_low = probs.astype(jnp.bfloat16)
    dprobs = jnp.einsum("rgd,kd->grk", upstream, value_part, preferred_element_type=jnp.float32)
    row_dot = jnp.sum(probs * dprobs, axis=2, keepdims=True)
    dscores = (probs * (dprobs - row_dot)).astype(jnp.bfloat16)
    grad_q = (
        jnp.einsum("grk,kd->rgd", dscores, key_part, preferred_element_type=jnp.float32)
        * score_scale
    ).astype(jnp.bfloat16)
    grad_k = (
        jnp.einsum("grk,rgd->kd", dscores, query_blk, preferred_element_type=jnp.float32)
        * score_scale
    )
    grad_v = jnp.einsum("grk,rgd->kd", probs_low, upstream, preferred_element_type=jnp.float32)
    return (grad_q.reshape(query_blk.shape[0], -1), jnp.concatenate([grad_k, grad_v], axis=1))


def shards(layer_input, queries, key_rows, value_rows, grad_output, segments, lengths):
    ctx_count = lax.axis_size("ctx")
    dp_count = lax.axis_size("dp")
    ctx_place = lax.axis_index("ctx")
    row_count = layer_input.shape[1]
    width_all = layer_input.shape[2]
    head_size = key_rows.shape[2]
    group_size = queries.shape[2] // head_size
    reach_count = min(8, ctx_count // 2)
    window_len = reach_count * row_count
    score_scale = 1.0 / math.sqrt(head_size)
    local_pair = jnp.concatenate([key_rows[0], value_rows[0]], axis=1)
    earlier = []
    for offset in range(1, reach_count + 1):
        earlier.append(passed_along(local_pair, "ctx", offset))
    key_all = jnp.concatenate(earlier[::-1] + [local_pair], axis=0)
    length = lengths[0]
    seg_row = segments[0]
    seg_pad = jnp.concatenate([jnp.full((window_len,), -1, jnp.int32), seg_row])
    first_row = ctx_place * row_count
    query_seg = lax.dynamic_slice_in_dim(seg_row, first_row, row_count, 0)
    key_seg = lax.dynamic_slice_in_dim(seg_pad, first_row, window_len + row_count, 0)
    query_pos = first_row + jnp.arange(row_count, dtype=jnp.int32)
    key_pos = first_row - window_len + jnp.arange(window_len + row_count, dtype=jnp.int32)
    allowed = make_mask(query_seg, key_seg, query_pos, key_pos, length, window_len)
    live = (query_pos < length).astype(jnp.float32)
    query_blk = queries[0].reshape(row_count, group_size, head_size)
    upstream = grad_output[0].reshape(row_count, group_size, head_size)
    grad_q, contrib = block_grads(query_blk, upstream, key_all, allowed, live, score_scale)
    blocks = contrib.reshape(reach_count + 1, row_count, 2 * head_size)
    total = blocks[reach_count]
    for offset in range(1, reach_count + 1):
        total = total + passed_along(blocks[reach_count - offset], "ctx", -offset)
    grad_kv = total.astype(jnp.bfloat16)
    slab_rows = width_all // (dp_count * ctx_count)
    inputs_flat = layer_input[0]
    partial_value = jnp.einsum(
        "rd,rc->dc", inputs_flat, grad_kv, preferred_element_type=jnp.float32
    )
    pieces = partial_value.reshape(dp_count, ctx_count, slab_rows, 2 * head_size)
    moved = lax.all_to_all(pieces, "ctx", split_axis=1, concat_axis=1, tiled=True)
    rollout_part = jnp.sum(moved, axis=1).reshape(dp_count * slab_rows, 2 * head_size)
    summed = lax.psum_scatter(rollout_part, "dp", scatter_dimension=0, tiled=True)
    grad_weights = (summed / dp_count).astype(jnp.bfloat16)
    return (grad_q.reshape(1, row_count, group_size * head_size), grad_weights)


def fused_kernel(
    n_dp, n_ctx, reach,
    x_ref, q_ref, k_ref, v_ref, go_ref, seg_ref, len_ref,
    gq_ref, gw_ref,
    kbuf, vbuf, qs, gos, bias, p_low, ds_low, gsend, grecv, gkv_t, xbuf, csend, crecv, zsend, zrecv,
    load_sem, xl_sem, kv_ss, kv_rs, g_ss, g_rs, a_ss, a_rs, x_ss, x_rs, c_ss, c_rs, z_ss, z_rs,
):
    rows = k_ref.shape[0]
    head = k_ref.shape[1]
    group = q_ref.shape[1] // head
    slab = gw_ref.shape[0]
    nz = n_dp // 2
    window = reach * rows
    scale = 1.0 / math.sqrt(head)
    dp = lax.axis_index("dp")
    ctx = lax.axis_index("ctx")
    z = dp // 2
    core = dp % 2
    sibling = z * 2 + (1 - core)

    def remote(src, dst, ss, rs, dp_to, ctx_to):
        return pltpu.make_async_remote_copy(
            src_ref=src, dst_ref=dst, send_sem=ss, recv_sem=rs,
            device_id={"dp": dp_to, "ctx": ctx_to}, device_id_type=pl.DeviceIdType.MESH,
        )

    loads = []
    for h in range(group):
        cols = pl.ds(h * head, head)
        loads.append(pltpu.make_async_copy(q_ref.at[:, cols], qs.at[pl.ds(h * rows, rows)], load_sem.at[2 * h]))
        loads.append(pltpu.make_async_copy(go_ref.at[:, cols], gos.at[pl.ds(h * rows, rows)], load_sem.at[2 * h + 1]))
    loads.append(pltpu.make_async_copy(k_ref, kbuf.at[pl.ds(window, rows)], load_sem.at[2 * group]))
    loads.append(pltpu.make_async_copy(v_ref, vbuf.at[pl.ds(window, rows)], load_sem.at[2 * group + 1]))
    for copy in loads:
        copy.start()

    barrier = pltpu.get_barrier_semaphore()
    for o in range(1, n_ctx):
        pl.semaphore_signal(barrier, inc=1, device_id={"dp": dp, "ctx": (ctx + o) % n_ctx}, device_id_type=pl.DeviceIdType.MESH)
    pl.semaphore_signal(barrier, inc=1, device_id={"dp": sibling, "ctx": ctx}, device_id_type=pl.DeviceIdType.MESH)
    for o in range(1, nz):
        pl.semaphore_signal(barrier, inc=1, device_id={"dp": ((z + o) % nz) * 2 + core, "ctx": ctx}, device_id_type=pl.DeviceIdType.MESH)
    pl.semaphore_wait(barrier, n_ctx - 1 + 1 + nz - 1)

    def kv_copies(off, to):
        slot = pl.ds((reach - off) * rows, rows)
        return (
            remote(k_ref, kbuf.at[slot], kv_ss.at[off - 1, 0], kv_rs.at[off - 1, 0], dp, to),
            remote(v_ref, vbuf.at[slot], kv_ss.at[off - 1, 1], kv_rs.at[off - 1, 1], dp, to),
        )

    for off in range(1, reach + 1):
        @pl.when(ctx + off < n_ctx)
        def _():
            for copy in kv_copies(off, (ctx + off) % n_ctx):
                copy.start()

    def piece_dp(k, s):
        return ((z + 1 + k) % nz) * 2 + (1 - core if s == 0 else core)

    def x_copy(k, s, o, source, to):
        d = piece_dp(k, s)
        cols = pl.ds(pl.multiple_of((d * n_ctx + to) * slab, slab), slab)
        return remote(
            x_ref.at[:, cols], xbuf.at[d, pl.ds(pl.multiple_of(source * rows, rows), rows)],
            x_ss.at[k, s, o - 1], x_rs.at[k, s, o - 1], dp, to,
        )

    def x_local(k, s):
        d = piece_dp(k, s)
        cols = pl.ds(pl.multiple_of((d * n_ctx + ctx) * slab, slab), slab)
        return pltpu.make_async_copy(
            x_ref.at[:, cols], xbuf.at[d, pl.ds(pl.multiple_of(ctx * rows, rows), rows)], xl_sem.at[k, s]
        )

    pieces = [(k, s) for k in range(nz) for s in range(2)]

    def issue(some):
        for k, s in some:
            for o in range(1, n_ctx):
                x_copy(k, s, o, ctx, (ctx + o) % n_ctx).start()
            x_local(k, s).start()

    issue(pieces[:3])

    length = len_ref[0]
    key_at = lax.broadcasted_iota(jnp.int32, (rows, rows), 0)
    query_at = lax.broadcasted_iota(jnp.int32, (rows, rows), 1) + ctx * rows
    query_seg = seg_ref[:, pl.ds(pl.multiple_of(ctx * rows, rows), rows)].astype(F32)
    for b in range(reach + 1):
        first = (ctx - (reach - b)) * rows
        from_row = pl.multiple_of(jnp.maximum(ctx - (reach - b), 0) * rows, rows)
        key_seg = jnp.broadcast_to(seg_ref[:, pl.ds(from_row, rows)].astype(F32), (rows, rows)).T
        key_pos = key_at + first
        gap = query_at - key_pos
        ok = (key_seg == query_seg) & (gap >= 0) & (gap < window) & (key_pos >= 0)
        ok = ok & ((key_pos < length) | (gap == 0))
        bias[pl.ds(b * rows, rows), :] = jnp.where(ok, 0.0, -1e30)
    live = (lax.broadcasted_iota(jnp.int32, (1, rows), 1) + ctx * rows < length).astype(F32)

    for off in range(1, reach + 1):
        slot = pl.ds((reach - off) * rows, rows)

        @pl.when(ctx - off < 0)
        def _():
            kbuf[slot, :] = jnp.zeros((rows, head), BF16)
            vbuf[slot, :] = jnp.zeros((rows, head), BF16)

    for copy in loads:
        copy.wait()
    for off in range(1, reach + 1):
        @pl.when(ctx - off >= 0)
        def _():
            for copy in kv_copies(off, ctx):
                copy.wait_recv()

    for h in range(group):
        if h == group // 2:
            issue(pieces[3:4])
        here = pl.ds(h * rows, rows)
        score = lax.dot_general(kbuf[...], qs[here, :], NT, preferred_element_type=F32) + bias[...]
        top = jnp.max(score, axis=0, keepdims=True)
        unnorm = jnp.exp2((score - top) * (scale * LOG2E))
        probs = unnorm * (live / jnp.sum(unnorm, axis=0, keepdims=True))
        p_low[:, here] = probs.astype(BF16)
        dprobs = lax.dot_general(vbuf[...], gos[here, :], NT, preferred_element_type=F32)
        row_dot = jnp.sum(probs * dprobs, axis=0, keepdims=True)
        ds_low[:, here] = (probs * (dprobs - row_dot)).astype(BF16)

    def kv_grad(b):
        block = pl.ds(b * rows, rows)
        gk = jnp.dot(ds_low[block, :], qs[...], preferred_element_type=F32) * scale
        gv = jnp.dot(p_low[block, :], gos[...], preferred_element_type=F32)
        return gk, gv

    def g_copy(off, to):
        return remote(gsend.at[off - 1], grecv.at[off - 1], g_ss.at[off - 1], g_rs.at[off - 1], dp, to)

    for off in range(1, reach + 1):
        gk, gv = kv_grad(reach - off)
        gsend[off - 1, :, pl.ds(0, head)] = gk.astype(BF16)
        gsend[off - 1, :, pl.ds(head, head)] = gv.astype(BF16)

        @pl.when(ctx - off >= 0)
        def _():
            g_copy(off, (ctx + n_ctx - off) % n_ctx).start()

        @pl.when(ctx + off >= n_ctx)
        def _():
            grecv[off - 1] = jnp.zeros((rows, 2 * head), BF16)

    issue(pieces[4:5])
    gk, gv = kv_grad(reach)

    key_t = kbuf[...].astype(F32).T.astype(BF16)
    for h in range(group):
        here = pl.ds(h * rows, rows)
        gq_t = jnp.dot(key_t, ds_low[:, here], preferred_element_type=F32) * scale
        gq_ref[:, pl.ds(h * head, head)] = gq_t.T.astype(BF16)

    for off in range(1, reach + 1):
        @pl.when(ctx + off < n_ctx)
        def _():
            g_copy(off, ctx).wait_recv()
    for off in range(1, reach + 1):
        gk = gk + grecv[off - 1, :, pl.ds(0, head)].astype(F32)
        gv = gv + grecv[off - 1, :, pl.ds(head, head)].astype(F32)
    own = pl.ds(pl.multiple_of(ctx * rows, rows), rows)
    gkv_t[pl.ds(0, head), own] = gk.T.astype(BF16)
    gkv_t[pl.ds(head, head), own] = gv.T.astype(BF16)

    def a_copy(o, source, to):
        part = gkv_t.at[:, pl.ds(pl.multiple_of(source * rows, rows), rows)]
        return remote(part, part, a_ss.at[o - 1], a_rs.at[o - 1], dp, to)

    for o in range(1, n_ctx):
        a_copy(o, ctx, (ctx + o) % n_ctx).start()
    issue(pieces[5:])
    for o in range(1, n_ctx):
        a_copy(o, (ctx + n_ctx - o) % n_ctx, ctx).wait_recv()

    def product(k, s):
        for o in range(1, n_ctx):
            x_copy(k, s, o, (ctx + n_ctx - o) % n_ctx, ctx).wait_recv()
        x_local(k, s).wait()
        return jnp.dot(gkv_t[...], xbuf[piece_dp(k, s)], preferred_element_type=F32)

    def c_copy(k):
        return remote(csend.at[k], crecv.at[k], c_ss.at[k], c_rs.at[k], sibling, ctx)

    def z_copy(k):
        return remote(zsend.at[k], zrecv.at[k], z_ss.at[k], z_rs.at[k], piece_dp(k, 1), ctx)

    def to_sibling(k):
        csend[k] = product(k, 0).astype(BF16)
        c_copy(k).start()

    total = None
    to_sibling(0)
    for k in range(nz):
        if k == 0:
            to_sibling(1)
        elif k > 1:
            to_sibling(k)
        part = product(k, 1)
        c_copy(k).wait_recv()
        part = part + crecv[k].astype(F32)
        if k < nz - 1:
            zsend[k] = part.astype(BF16)
            z_copy(k).start()
        else:
            total = part
    for k in range(nz - 1):
        z_copy(k).wait_recv()
        total = total + zrecv[k].astype(F32)
    gw_ref[...] = (total * (1.0 / n_dp)).T.astype(BF16)

    for off in range(1, reach + 1):
        @pl.when(ctx + off < n_ctx)
        def _():
            for copy in kv_copies(off, (ctx + off) % n_ctx):
                copy.wait_send()

        @pl.when(ctx - off >= 0)
        def _():
            g_copy(off, (ctx + n_ctx - off) % n_ctx).wait_send()
    for o in range(1, n_ctx):
        a_copy(o, ctx, (ctx + o) % n_ctx).wait_send()
    for k in range(nz):
        for s in range(2):
            for o in range(1, n_ctx):
                x_copy(k, s, o, ctx, (ctx + o) % n_ctx).wait_send()
        c_copy(k).wait_send()
        if k < nz - 1:
            z_copy(k).wait_send()


def fused_shards(layer_input, queries, key_rows, value_rows, grad_output, segments, lengths):
    n_dp = lax.axis_size("dp")
    n_ctx = lax.axis_size("ctx")
    rows, width = layer_input.shape[1:]
    head = key_rows.shape[2]
    group = queries.shape[2] // head
    reach = min(8, n_ctx // 2)
    keys = (reach + 1) * rows
    slab = width // (n_dp * n_ctx)
    nz = n_dp // 2
    dma = pltpu.SemaphoreType.DMA
    hbm = pl.BlockSpec(memory_space=pltpu.HBM)
    vmem = pl.BlockSpec(memory_space=pltpu.VMEM)
    smem = pl.BlockSpec(memory_space=pltpu.SMEM)
    gq, gw = pl.pallas_call(
        functools.partial(fused_kernel, n_dp, n_ctx, reach),
        out_shape=(
            jax.ShapeDtypeStruct((rows, group * head), BF16),
            jax.ShapeDtypeStruct((slab, 2 * head), BF16),
        ),
        in_specs=[hbm] * 5 + [vmem, smem],
        out_specs=(vmem, vmem),
        scratch_shapes=[
            pltpu.VMEM((keys, head), BF16),
            pltpu.VMEM((keys, head), BF16),
            pltpu.VMEM((group * rows, head), BF16),
            pltpu.VMEM((group * rows, head), BF16),
            pltpu.VMEM((keys, rows), F32),
            pltpu.VMEM((keys, group * rows), BF16),
            pltpu.VMEM((keys, group * rows), BF16),
            pltpu.VMEM((reach, rows, 2 * head), BF16),
            pltpu.VMEM((reach, rows, 2 * head), BF16),
            pltpu.VMEM((2 * head, n_ctx * rows), BF16),
            pltpu.VMEM((n_dp, n_ctx * rows, slab), BF16),
            pltpu.VMEM((nz, 2 * head, slab), BF16),
            pltpu.VMEM((nz, 2 * head, slab), BF16),
            pltpu.VMEM((nz - 1, 2 * head, slab), BF16),
            pltpu.VMEM((nz - 1, 2 * head, slab), BF16),
            dma((2 * group + 2,)),
            dma((nz, 2)),
            dma((reach, 2)),
            dma((reach, 2)),
            dma((reach,)),
            dma((reach,)),
            dma((n_ctx - 1,)),
            dma((n_ctx - 1,)),
            dma((nz, 2, n_ctx - 1)),
            dma((nz, 2, n_ctx - 1)),
            dma((nz,)),
            dma((nz,)),
            dma((nz - 1,)),
            dma((nz - 1,)),
        ],
        compiler_params=pltpu.CompilerParams(
            collective_id=0, has_side_effects=True, vmem_limit_bytes=62 * 1024 * 1024
        ),
    )(layer_input[0], queries[0], key_rows[0], value_rows[0], grad_output[0], segments, lengths)
    return gq[None], gw


def by_size(layer_input, *rest):
    n_dp, n_ctx = lax.axis_size("dp"), lax.axis_size("ctx")
    slab = layer_input.shape[2] // (n_dp * n_ctx)
    whole_tiles = slab % 128 == 0 and layer_input.shape[1] % 128 == 0
    run = fused_shards if whole_tiles and n_dp % 2 == 0 and n_dp > 2 else shards
    return run(layer_input, *rest)


def solution(mesh):
    return jax.shard_map(
        by_size,
        mesh=mesh,
        in_specs=(
            P("dp", "ctx", None),
            P("dp", "ctx", None),
            P("dp", "ctx", None),
            P("dp", "ctx", None),
            P("dp", "ctx", None),
            P("dp", None),
            P("dp"),
        ),
        out_specs=(P("dp", "ctx", None), P(("dp", "ctx"), None)),
        check_vma=False,
    )
```

```python
import functools
import math

import jax
import jax.numpy as jnp
from jax import lax
from jax.experimental import pallas as pl
from jax.experimental.pallas import tpu as pltpu
from jax.sharding import PartitionSpec as P

F32 = jnp.float32
BF16 = jnp.bfloat16
LOG2E = 1.4426950408889634
NT = (((1,), (1,)), ((), ()))


def passed_along(x, axis, by):
    length = lax.axis_size(axis)
    pairs = [(i, i + by) for i in range(length) if 0 <= i + by < length]
    return lax.ppermute(x, axis, pairs)


def make_mask(query_seg, key_seg, query_pos, key_pos, length, window_len):
    gap = query_pos[:, None] - key_pos[None, :]
    same_doc = query_seg[:, None] == key_seg[None, :]
    inside = (gap >= 0) & (gap < window_len)
    alive = (key_pos[None, :] < length) | (gap == 0)
    return same_doc & inside & alive


def block_grads(query_blk, upstream, key_all, allowed, live, score_scale):
    head_size = key_all.shape[1] // 2
    key_part = key_all[:, :head_size]
    value_part = key_all[:, head_size:]
    scores = (
        jnp.einsum("rgd,kd->grk", query_blk, key_part, preferred_element_type=jnp.float32)
        * score_scale
    )
    masked = jnp.where(allowed[None], scores, -1e30)
    row_max = jnp.max(masked, axis=2, keepdims=True)
    unnorm = jnp.where(allowed[None], jnp.exp(masked - row_max), 0.0)
    probs = unnorm / jnp.sum(unnorm, axis=2, keepdims=True) * live[None, :, None]
    probs_low = probs.astype(jnp.bfloat16)
    dprobs = jnp.einsum("rgd,kd->grk", upstream, value_part, preferred_element_type=jnp.float32)
    row_dot = jnp.sum(probs * dprobs, axis=2, keepdims=True)
    dscores = (probs * (dprobs - row_dot)).astype(jnp.bfloat16)
    grad_q = (
        jnp.einsum("grk,kd->rgd", dscores, key_part, preferred_element_type=jnp.float32)
        * score_scale
    ).astype(jnp.bfloat16)
    grad_k = (
        jnp.einsum("grk,rgd->kd", dscores, query_blk, preferred_element_type=jnp.float32)
        * score_scale
    )
    grad_v = jnp.einsum("grk,rgd->kd", probs_low, upstream, preferred_element_type=jnp.float32)
    return (grad_q.reshape(query_blk.shape[0], -1), jnp.concatenate([grad_k, grad_v], axis=1))


def shards(layer_input, queries, key_rows, value_rows, grad_output, segments, lengths):
    ctx_count = lax.axis_size("ctx")
    dp_count = lax.axis_size("dp")
    ctx_place = lax.axis_index("ctx")
    row_count = layer_input.shape[1]
    width_all = layer_input.shape[2]
    head_size = key_rows.shape[2]
    group_size = queries.shape[2] // head_size
    reach_count = min(8, ctx_count // 2)
    window_len = reach_count * row_count
    score_scale = 1.0 / math.sqrt(head_size)
    local_pair = jnp.concatenate([key_rows[0], value_rows[0]], axis=1)
    earlier = []
    for offset in range(1, reach_count + 1):
        earlier.append(passed_along(local_pair, "ctx", offset))
    key_all = jnp.concatenate(earlier[::-1] + [local_pair], axis=0)
    length = lengths[0]
    seg_row = segments[0]
    seg_pad = jnp.concatenate([jnp.full((window_len,), -1, jnp.int32), seg_row])
    first_row = ctx_place * row_count
    query_seg = lax.dynamic_slice_in_dim(seg_row, first_row, row_count, 0)
    key_seg = lax.dynamic_slice_in_dim(seg_pad, first_row, window_len + row_count, 0)
    query_pos = first_row + jnp.arange(row_count, dtype=jnp.int32)
    key_pos = first_row - window_len + jnp.arange(window_len + row_count, dtype=jnp.int32)
    allowed = make_mask(query_seg, key_seg, query_pos, key_pos, length, window_len)
    live = (query_pos < length).astype(jnp.float32)
    query_blk = queries[0].reshape(row_count, group_size, head_size)
    upstream = grad_output[0].reshape(row_count, group_size, head_size)
    grad_q, contrib = block_grads(query_blk, upstream, key_all, allowed, live, score_scale)
    blocks = contrib.reshape(reach_count + 1, row_count, 2 * head_size)
    total = blocks[reach_count]
    for offset in range(1, reach_count + 1):
        total = total + passed_along(blocks[reach_count - offset], "ctx", -offset)
    grad_kv = total.astype(jnp.bfloat16)
    slab_rows = width_all // (dp_count * ctx_count)
    inputs_flat = layer_input[0]
    partial_value = jnp.einsum(
        "rd,rc->dc", inputs_flat, grad_kv, preferred_element_type=jnp.float32
    )
    pieces = partial_value.reshape(dp_count, ctx_count, slab_rows, 2 * head_size)
    moved = lax.all_to_all(pieces, "ctx", split_axis=1, concat_axis=1, tiled=True)
    rollout_part = jnp.sum(moved, axis=1).reshape(dp_count * slab_rows, 2 * head_size)
    summed = lax.psum_scatter(rollout_part, "dp", scatter_dimension=0, tiled=True)
    grad_weights = (summed / dp_count).astype(jnp.bfloat16)
    return (grad_q.reshape(1, row_count, group_size * head_size), grad_weights)


def fused_kernel(
    n_dp, n_ctx, reach,
    x_ref, q_ref, k_ref, v_ref, go_ref, seg_ref, len_ref,
    gq_ref, gw_ref,
    kbuf, vbuf, qs, gos, bias, p_low, ds_low, gsend, grecv, gkv_t, xbuf, csend, crecv, zsend, zrecv,
    load_sem, xl_sem, kv_ss, kv_rs, g_ss, g_rs, a_ss, a_rs, x_ss, x_rs, c_ss, c_rs, z_ss, z_rs,
):
    rows = k_ref.shape[0]
    head = k_ref.shape[1]
    group = q_ref.shape[1] // head
    slab = gw_ref.shape[0]
    nz = n_dp // 2
    window = reach * rows
    scale = 1.0 / math.sqrt(head)
    dp = lax.axis_index("dp")
    ctx = lax.axis_index("ctx")
    z = dp // 2
    core = dp % 2
    sibling = z * 2 + (1 - core)

    def remote(src, dst, ss, rs, dp_to, ctx_to):
        return pltpu.make_async_remote_copy(
            src_ref=src, dst_ref=dst, send_sem=ss, recv_sem=rs,
            device_id={"dp": dp_to, "ctx": ctx_to}, device_id_type=pl.DeviceIdType.MESH,
        )

    loads = []
    for h in range(group):
        cols = pl.ds(h * head, head)
        loads.append(pltpu.make_async_copy(q_ref.at[:, cols], qs.at[pl.ds(h * rows, rows)], load_sem.at[2 * h]))
        loads.append(pltpu.make_async_copy(go_ref.at[:, cols], gos.at[pl.ds(h * rows, rows)], load_sem.at[2 * h + 1]))
    loads.append(pltpu.make_async_copy(k_ref, kbuf.at[pl.ds(window, rows)], load_sem.at[2 * group]))
    loads.append(pltpu.make_async_copy(v_ref, vbuf.at[pl.ds(window, rows)], load_sem.at[2 * group + 1]))
    for copy in loads:
        copy.start()

    barrier = pltpu.get_barrier_semaphore()
    for o in range(1, n_ctx):
        pl.semaphore_signal(barrier, inc=1, device_id={"dp": dp, "ctx": (ctx + o) % n_ctx}, device_id_type=pl.DeviceIdType.MESH)
    pl.semaphore_signal(barrier, inc=1, device_id={"dp": sibling, "ctx": ctx}, device_id_type=pl.DeviceIdType.MESH)
    for o in range(1, nz):
        pl.semaphore_signal(barrier, inc=1, device_id={"dp": ((z + o) % nz) * 2 + core, "ctx": ctx}, device_id_type=pl.DeviceIdType.MESH)
    pl.semaphore_wait(barrier, n_ctx - 1 + 1 + nz - 1)

    def kv_copies(off, to):
        slot = pl.ds((reach - off) * rows, rows)
        return (
            remote(k_ref, kbuf.at[slot], kv_ss.at[off - 1, 0], kv_rs.at[off - 1, 0], dp, to),
            remote(v_ref, vbuf.at[slot], kv_ss.at[off - 1, 1], kv_rs.at[off - 1, 1], dp, to),
        )

    for off in range(1, reach + 1):
        @pl.when(ctx + off < n_ctx)
        def _():
            for copy in kv_copies(off, (ctx + off) % n_ctx):
                copy.start()

    def piece_dp(k, s):
        return ((z + 1 + k) % nz) * 2 + (1 - core if s == 0 else core)

    def x_copy(k, s, o, source, to):
        d = piece_dp(k, s)
        cols = pl.ds(pl.multiple_of((d * n_ctx + to) * slab, slab), slab)
        return remote(
            x_ref.at[:, cols], xbuf.at[d, pl.ds(pl.multiple_of(source * rows, rows), rows)],
            x_ss.at[k, s, o - 1], x_rs.at[k, s, o - 1], dp, to,
        )

    def x_local(k, s):
        d = piece_dp(k, s)
        cols = pl.ds(pl.multiple_of((d * n_ctx + ctx) * slab, slab), slab)
        return pltpu.make_async_copy(
            x_ref.at[:, cols], xbuf.at[d, pl.ds(pl.multiple_of(ctx * rows, rows), rows)], xl_sem.at[k, s]
        )

    pieces = [(k, s) for k in range(nz) for s in range(2)]

    def issue(some):
        for k, s in some:
            for o in range(1, n_ctx):
                x_copy(k, s, o, ctx, (ctx + o) % n_ctx).start()
            x_local(k, s).start()

    issue(pieces[:1])

    length = len_ref[0]
    key_at = lax.broadcasted_iota(jnp.int32, (rows, rows), 0)
    query_at = lax.broadcasted_iota(jnp.int32, (rows, rows), 1) + ctx * rows
    query_seg = seg_ref[:, pl.ds(pl.multiple_of(ctx * rows, rows), rows)].astype(F32)
    for b in range(reach + 1):
        first = (ctx - (reach - b)) * rows
        from_row = pl.multiple_of(jnp.maximum(ctx - (reach - b), 0) * rows, rows)
        key_seg = jnp.broadcast_to(seg_ref[:, pl.ds(from_row, rows)].astype(F32), (rows, rows)).T
        key_pos = key_at + first
        gap = query_at - key_pos
        ok = (key_seg == query_seg) & (gap >= 0) & (gap < window) & (key_pos >= 0)
        ok = ok & ((key_pos < length) | (gap == 0))
        bias[pl.ds(b * rows, rows), :] = jnp.where(ok, 0.0, -1e30)
    live = (lax.broadcasted_iota(jnp.int32, (1, rows), 1) + ctx * rows < length).astype(F32)

    for off in range(1, reach + 1):
        slot = pl.ds((reach - off) * rows, rows)

        @pl.when(ctx - off < 0)
        def _():
            kbuf[slot, :] = jnp.zeros((rows, head), BF16)
            vbuf[slot, :] = jnp.zeros((rows, head), BF16)

    for copy in loads:
        copy.wait()
    for off in range(1, reach + 1):
        @pl.when(ctx - off >= 0)
        def _():
            for copy in kv_copies(off, ctx):
                copy.wait_recv()

    for h in range(group):
        if h == group // 2:
            issue(pieces[1:2])
        here = pl.ds(h * rows, rows)
        score = lax.dot_general(kbuf[...], qs[here, :], NT, preferred_element_type=F32) + bias[...]
        top = jnp.max(score, axis=0, keepdims=True)
        unnorm = jnp.exp2((score - top) * (scale * LOG2E))
        probs = unnorm * (live / jnp.sum(unnorm, axis=0, keepdims=True))
        p_low[:, here] = probs.astype(BF16)
        dprobs = lax.dot_general(vbuf[...], gos[here, :], NT, preferred_element_type=F32)
        row_dot = jnp.sum(probs * dprobs, axis=0, keepdims=True)
        ds_low[:, here] = (probs * (dprobs - row_dot)).astype(BF16)

    def kv_grad(b):
        block = pl.ds(b * rows, rows)
        gk = jnp.dot(ds_low[block, :], qs[...], preferred_element_type=F32) * scale
        gv = jnp.dot(p_low[block, :], gos[...], preferred_element_type=F32)
        return gk, gv

    def g_copy(off, to):
        return remote(gsend.at[off - 1], grecv.at[off - 1], g_ss.at[off - 1], g_rs.at[off - 1], dp, to)

    for off in range(1, reach + 1):
        gk, gv = kv_grad(reach - off)
        gsend[off - 1, :, pl.ds(0, head)] = gk.astype(BF16)
        gsend[off - 1, :, pl.ds(head, head)] = gv.astype(BF16)

        @pl.when(ctx - off >= 0)
        def _():
            g_copy(off, (ctx + n_ctx - off) % n_ctx).start()

        @pl.when(ctx + off >= n_ctx)
        def _():
            grecv[off - 1] = jnp.zeros((rows, 2 * head), BF16)

    issue(pieces[2:3])
    gk, gv = kv_grad(reach)

    key_t = kbuf[...].astype(F32).T.astype(BF16)
    for h in range(group):
        here = pl.ds(h * rows, rows)
        gq_t = jnp.dot(key_t, ds_low[:, here], preferred_element_type=F32) * scale
        gq_ref[:, pl.ds(h * head, head)] = gq_t.T.astype(BF16)

    for off in range(1, reach + 1):
        @pl.when(ctx + off < n_ctx)
        def _():
            g_copy(off, ctx).wait_recv()
    for off in range(1, reach + 1):
        gk = gk + grecv[off - 1, :, pl.ds(0, head)].astype(F32)
        gv = gv + grecv[off - 1, :, pl.ds(head, head)].astype(F32)
    own = pl.ds(pl.multiple_of(ctx * rows, rows), rows)
    gkv_t[pl.ds(0, head), own] = gk.T.astype(BF16)
    gkv_t[pl.ds(head, head), own] = gv.T.astype(BF16)

    def a_copy(o, source, to):
        part = gkv_t.at[:, pl.ds(pl.multiple_of(source * rows, rows), rows)]
        return remote(part, part, a_ss.at[o - 1], a_rs.at[o - 1], dp, to)

    for o in range(1, n_ctx):
        a_copy(o, ctx, (ctx + o) % n_ctx).start()
    issue(pieces[3:])
    for o in range(1, n_ctx):
        a_copy(o, (ctx + n_ctx - o) % n_ctx, ctx).wait_recv()

    def product(k, s):
        for o in range(1, n_ctx):
            x_copy(k, s, o, (ctx + n_ctx - o) % n_ctx, ctx).wait_recv()
        x_local(k, s).wait()
        return jnp.dot(gkv_t[...], xbuf[piece_dp(k, s)], preferred_element_type=F32)

    def c_copy(k):
        return remote(csend.at[k], crecv.at[k], c_ss.at[k], c_rs.at[k], sibling, ctx)

    def z_copy(k):
        return remote(zsend.at[k], zrecv.at[k], z_ss.at[k], z_rs.at[k], piece_dp(k, 1), ctx)

    def to_sibling(k):
        csend[k] = product(k, 0).astype(BF16)
        c_copy(k).start()

    total = None
    to_sibling(0)
    for k in range(nz):
        if k == 0:
            to_sibling(1)
        elif k > 1:
            to_sibling(k)
        part = product(k, 1)
        c_copy(k).wait_recv()
        part = part + crecv[k].astype(F32)
        if k < nz - 1:
            zsend[k] = part.astype(BF16)
            z_copy(k).start()
        else:
            total = part
    for k in range(nz - 1):
        z_copy(k).wait_recv()
        total = total + zrecv[k].astype(F32)
    gw_ref[...] = (total * (1.0 / n_dp)).T.astype(BF16)

    for off in range(1, reach + 1):
        @pl.when(ctx + off < n_ctx)
        def _():
            for copy in kv_copies(off, (ctx + off) % n_ctx):
                copy.wait_send()

        @pl.when(ctx - off >= 0)
        def _():
            g_copy(off, (ctx + n_ctx - off) % n_ctx).wait_send()
    for o in range(1, n_ctx):
        a_copy(o, ctx, (ctx + o) % n_ctx).wait_send()
    for k in range(nz):
        for s in range(2):
            for o in range(1, n_ctx):
                x_copy(k, s, o, ctx, (ctx + o) % n_ctx).wait_send()
        c_copy(k).wait_send()
        if k < nz - 1:
            z_copy(k).wait_send()


def hand_over(gq_from, gw_from, gq_to, gw_to, sem):
    copies = [
        pltpu.make_async_copy(gq_from, gq_to, sem.at[0]),
        pltpu.make_async_copy(gw_from, gw_to, sem.at[1]),
    ]
    for copy in copies:
        copy.start()
    for copy in copies:
        copy.wait()


def fused_shards(layer_input, queries, key_rows, value_rows, grad_output, segments, lengths):
    n_dp = lax.axis_size("dp")
    n_ctx = lax.axis_size("ctx")
    rows, width = layer_input.shape[1:]
    head = key_rows.shape[2]
    group = queries.shape[2] // head
    reach = min(8, n_ctx // 2)
    keys = (reach + 1) * rows
    slab = width // (n_dp * n_ctx)
    nz = n_dp // 2
    dma = pltpu.SemaphoreType.DMA
    hbm = pl.BlockSpec(memory_space=pltpu.HBM)
    vmem = pl.BlockSpec(memory_space=pltpu.VMEM)
    smem = pl.BlockSpec(memory_space=pltpu.SMEM)
    gq, gw = pl.pallas_call(
        functools.partial(fused_kernel, n_dp, n_ctx, reach),
        out_shape=(
            jax.ShapeDtypeStruct((rows, group * head), BF16),
            jax.ShapeDtypeStruct((slab, 2 * head), BF16),
        ),
        in_specs=[hbm] * 5 + [vmem, smem],
        out_specs=(vmem, vmem),
        scratch_shapes=[
            pltpu.VMEM((keys, head), BF16),
            pltpu.VMEM((keys, head), BF16),
            pltpu.VMEM((group * rows, head), BF16),
            pltpu.VMEM((group * rows, head), BF16),
            pltpu.VMEM((keys, rows), F32),
            pltpu.VMEM((keys, group * rows), BF16),
            pltpu.VMEM((keys, group * rows), BF16),
            pltpu.VMEM((reach, rows, 2 * head), BF16),
            pltpu.VMEM((reach, rows, 2 * head), BF16),
            pltpu.VMEM((2 * head, n_ctx * rows), BF16),
            pltpu.VMEM((n_dp, n_ctx * rows, slab), BF16),
            pltpu.VMEM((nz, 2 * head, slab), BF16),
            pltpu.VMEM((nz, 2 * head, slab), BF16),
            pltpu.VMEM((nz - 1, 2 * head, slab), BF16),
            pltpu.VMEM((nz - 1, 2 * head, slab), BF16),
            dma((2 * group + 2,)),
            dma((nz, 2)),
            dma((reach, 2)),
            dma((reach, 2)),
            dma((reach,)),
            dma((reach,)),
            dma((n_ctx - 1,)),
            dma((n_ctx - 1,)),
            dma((nz, 2, n_ctx - 1)),
            dma((nz, 2, n_ctx - 1)),
            dma((nz,)),
            dma((nz,)),
            dma((nz - 1,)),
            dma((nz - 1,)),
        ],
        compiler_params=pltpu.CompilerParams(
            collective_id=0, has_side_effects=True, vmem_limit_bytes=62 * 1024 * 1024
        ),
    )(layer_input[0], queries[0], key_rows[0], value_rows[0], grad_output[0], segments, lengths)
    gq, gw = pl.pallas_call(
        hand_over,
        out_shape=(jax.ShapeDtypeStruct(gq.shape, BF16), jax.ShapeDtypeStruct(gw.shape, BF16)),
        in_specs=[hbm] * 2,
        out_specs=(hbm, hbm),
        scratch_shapes=[dma((2,))],
        compiler_params=pltpu.CompilerParams(vmem_limit_bytes=62 * 1024 * 1024),
    )(gq, gw)
    return gq[None], gw


def by_size(layer_input, *rest):
    n_dp, n_ctx = lax.axis_size("dp"), lax.axis_size("ctx")
    slab = layer_input.shape[2] // (n_dp * n_ctx)
    whole_tiles = slab % 128 == 0 and layer_input.shape[1] % 128 == 0
    run = fused_shards if whole_tiles and n_dp % 2 == 0 and n_dp > 2 else shards
    return run(layer_input, *rest)


def solution(mesh):
    return jax.shard_map(
        by_size,
        mesh=mesh,
        in_specs=(
            P("dp", "ctx", None),
            P("dp", "ctx", None),
            P("dp", "ctx", None),
            P("dp", "ctx", None),
            P("dp", "ctx", None),
            P("dp", None),
            P("dp"),
        ),
        out_specs=(P("dp", "ctx", None), P(("dp", "ctx"), None)),
        check_vma=False,
    )
```

```python
import functools
import math

import jax
import jax.numpy as jnp
from jax import lax
from jax.experimental import pallas as pl
from jax.experimental.pallas import tpu as pltpu
from jax.sharding import PartitionSpec as P

F32 = jnp.float32
BF16 = jnp.bfloat16
LOG2E = 1.4426950408889634
NT = (((1,), (1,)), ((), ()))


def passed_along(x, axis, by):
    length = lax.axis_size(axis)
    pairs = [(i, i + by) for i in range(length) if 0 <= i + by < length]
    return lax.ppermute(x, axis, pairs)


def make_mask(query_seg, key_seg, query_pos, key_pos, length, window_len):
    gap = query_pos[:, None] - key_pos[None, :]
    same_doc = query_seg[:, None] == key_seg[None, :]
    inside = (gap >= 0) & (gap < window_len)
    alive = (key_pos[None, :] < length) | (gap == 0)
    return same_doc & inside & alive


def block_grads(query_blk, upstream, key_all, allowed, live, score_scale):
    head_size = key_all.shape[1] // 2
    key_part = key_all[:, :head_size]
    value_part = key_all[:, head_size:]
    scores = (
        jnp.einsum("rgd,kd->grk", query_blk, key_part, preferred_element_type=jnp.float32)
        * score_scale
    )
    masked = jnp.where(allowed[None], scores, -1e30)
    row_max = jnp.max(masked, axis=2, keepdims=True)
    unnorm = jnp.where(allowed[None], jnp.exp(masked - row_max), 0.0)
    probs = unnorm / jnp.sum(unnorm, axis=2, keepdims=True) * live[None, :, None]
    probs_low = probs.astype(jnp.bfloat16)
    dprobs = jnp.einsum("rgd,kd->grk", upstream, value_part, preferred_element_type=jnp.float32)
    row_dot = jnp.sum(probs * dprobs, axis=2, keepdims=True)
    dscores = (probs * (dprobs - row_dot)).astype(jnp.bfloat16)
    grad_q = (
        jnp.einsum("grk,kd->rgd", dscores, key_part, preferred_element_type=jnp.float32)
        * score_scale
    ).astype(jnp.bfloat16)
    grad_k = (
        jnp.einsum("grk,rgd->kd", dscores, query_blk, preferred_element_type=jnp.float32)
        * score_scale
    )
    grad_v = jnp.einsum("grk,rgd->kd", probs_low, upstream, preferred_element_type=jnp.float32)
    return (grad_q.reshape(query_blk.shape[0], -1), jnp.concatenate([grad_k, grad_v], axis=1))


def shards(layer_input, queries, key_rows, value_rows, grad_output, segments, lengths):
    ctx_count = lax.axis_size("ctx")
    dp_count = lax.axis_size("dp")
    ctx_place = lax.axis_index("ctx")
    row_count = layer_input.shape[1]
    width_all = layer_input.shape[2]
    head_size = key_rows.shape[2]
    group_size = queries.shape[2] // head_size
    reach_count = min(8, ctx_count // 2)
    window_len = reach_count * row_count
    score_scale = 1.0 / math.sqrt(head_size)
    local_pair = jnp.concatenate([key_rows[0], value_rows[0]], axis=1)
    earlier = []
    for offset in range(1, reach_count + 1):
        earlier.append(passed_along(local_pair, "ctx", offset))
    key_all = jnp.concatenate(earlier[::-1] + [local_pair], axis=0)
    length = lengths[0]
    seg_row = segments[0]
    seg_pad = jnp.concatenate([jnp.full((window_len,), -1, jnp.int32), seg_row])
    first_row = ctx_place * row_count
    query_seg = lax.dynamic_slice_in_dim(seg_row, first_row, row_count, 0)
    key_seg = lax.dynamic_slice_in_dim(seg_pad, first_row, window_len + row_count, 0)
    query_pos = first_row + jnp.arange(row_count, dtype=jnp.int32)
    key_pos = first_row - window_len + jnp.arange(window_len + row_count, dtype=jnp.int32)
    allowed = make_mask(query_seg, key_seg, query_pos, key_pos, length, window_len)
    live = (query_pos < length).astype(jnp.float32)
    query_blk = queries[0].reshape(row_count, group_size, head_size)
    upstream = grad_output[0].reshape(row_count, group_size, head_size)
    grad_q, contrib = block_grads(query_blk, upstream, key_all, allowed, live, score_scale)
    blocks = contrib.reshape(reach_count + 1, row_count, 2 * head_size)
    total = blocks[reach_count]
    for offset in range(1, reach_count + 1):
        total = total + passed_along(blocks[reach_count - offset], "ctx", -offset)
    grad_kv = total.astype(jnp.bfloat16)
    slab_rows = width_all // (dp_count * ctx_count)
    inputs_flat = layer_input[0]
    partial_value = jnp.einsum(
        "rd,rc->dc", inputs_flat, grad_kv, preferred_element_type=jnp.float32
    )
    pieces = partial_value.reshape(dp_count, ctx_count, slab_rows, 2 * head_size)
    moved = lax.all_to_all(pieces, "ctx", split_axis=1, concat_axis=1, tiled=True)
    rollout_part = jnp.sum(moved, axis=1).reshape(dp_count * slab_rows, 2 * head_size)
    summed = lax.psum_scatter(rollout_part, "dp", scatter_dimension=0, tiled=True)
    grad_weights = (summed / dp_count).astype(jnp.bfloat16)
    return (grad_q.reshape(1, row_count, group_size * head_size), grad_weights)


def fused_kernel(
    n_dp, n_ctx, reach,
    x_ref, q_ref, k_ref, v_ref, go_ref, seg_ref, len_ref,
    gq_ref, gw_ref,
    xin, kbuf, vbuf, qs, gos, bias, p_low, ds_low, gsend, grecv, gkv_t, xbuf, csend, crecv, zsend, zrecv,
    xin_sem, load_sem, xl_sem, kv_ss, kv_rs, g_ss, g_rs, a_ss, a_rs, x_ss, x_rs, c_ss, c_rs, z_ss, z_rs,
):
    rows = k_ref.shape[0]
    head = k_ref.shape[1]
    group = q_ref.shape[1] // head
    slab = gw_ref.shape[0]
    nz = n_dp // 2
    window = reach * rows
    scale = 1.0 / math.sqrt(head)
    dp = lax.axis_index("dp")
    ctx = lax.axis_index("ctx")
    z = dp // 2
    core = dp % 2
    sibling = z * 2 + (1 - core)

    def remote(src, dst, ss, rs, dp_to, ctx_to):
        return pltpu.make_async_remote_copy(
            src_ref=src, dst_ref=dst, send_sem=ss, recv_sem=rs,
            device_id={"dp": dp_to, "ctx": ctx_to}, device_id_type=pl.DeviceIdType.MESH,
        )

    loads = []
    for h in range(group):
        cols = pl.ds(h * head, head)
        loads.append(pltpu.make_async_copy(q_ref.at[:, cols], qs.at[pl.ds(h * rows, rows)], load_sem.at[2 * h]))
        loads.append(pltpu.make_async_copy(go_ref.at[:, cols], gos.at[pl.ds(h * rows, rows)], load_sem.at[2 * h + 1]))
    loads.append(pltpu.make_async_copy(k_ref, kbuf.at[pl.ds(window, rows)], load_sem.at[2 * group]))
    loads.append(pltpu.make_async_copy(v_ref, vbuf.at[pl.ds(window, rows)], load_sem.at[2 * group + 1]))
    for copy in loads:
        copy.start()

    def x_load(k):
        wide = 2 * n_ctx * slab
        cols = pl.ds(pl.multiple_of(((z + 1 + k) % nz) * wide, wide), wide)
        return pltpu.make_async_copy(x_ref.at[:, cols], xin.at[:, cols], xin_sem.at[k])

    for k in range(nz):
        x_load(k).start()

    barrier = pltpu.get_barrier_semaphore()
    for o in range(1, n_ctx):
        pl.semaphore_signal(barrier, inc=1, device_id={"dp": dp, "ctx": (ctx + o) % n_ctx}, device_id_type=pl.DeviceIdType.MESH)
    pl.semaphore_signal(barrier, inc=1, device_id={"dp": sibling, "ctx": ctx}, device_id_type=pl.DeviceIdType.MESH)
    for o in range(1, nz):
        pl.semaphore_signal(barrier, inc=1, device_id={"dp": ((z + o) % nz) * 2 + core, "ctx": ctx}, device_id_type=pl.DeviceIdType.MESH)
    pl.semaphore_wait(barrier, n_ctx - 1 + 1 + nz - 1)

    def kv_copies(off, to):
        slot = pl.ds((reach - off) * rows, rows)
        return (
            remote(k_ref, kbuf.at[slot], kv_ss.at[off - 1, 0], kv_rs.at[off - 1, 0], dp, to),
            remote(v_ref, vbuf.at[slot], kv_ss.at[off - 1, 1], kv_rs.at[off - 1, 1], dp, to),
        )

    for off in range(1, reach + 1):
        @pl.when(ctx + off < n_ctx)
        def _():
            for copy in kv_copies(off, (ctx + off) % n_ctx):
                copy.start()

    def piece_dp(k, s):
        return ((z + 1 + k) % nz) * 2 + (1 - core if s == 0 else core)

    def x_copy(k, s, o, source, to):
        d = piece_dp(k, s)
        cols = pl.ds(pl.multiple_of((d * n_ctx + to) * slab, slab), slab)
        return remote(
            xin.at[:, cols], xbuf.at[d, pl.ds(pl.multiple_of(source * rows, rows), rows)],
            x_ss.at[k, s, o - 1], x_rs.at[k, s, o - 1], dp, to,
        )

    def x_local(k, s):
        d = piece_dp(k, s)
        cols = pl.ds(pl.multiple_of((d * n_ctx + ctx) * slab, slab), slab)
        return pltpu.make_async_copy(
            xin.at[:, cols], xbuf.at[d, pl.ds(pl.multiple_of(ctx * rows, rows), rows)], xl_sem.at[k, s]
        )

    pieces = [(k, s) for k in range(nz) for s in range(2)]

    def issue(some):
        for k, s in some:
            if s == 0:
                x_load(k).wait()
            for o in range(1, n_ctx):
                x_copy(k, s, o, ctx, (ctx + o) % n_ctx).start()
            x_local(k, s).start()

    issue(pieces[:2])

    length = len_ref[0]
    key_at = lax.broadcasted_iota(jnp.int32, (rows, rows), 0)
    query_at = lax.broadcasted_iota(jnp.int32, (rows, rows), 1) + ctx * rows
    query_seg = seg_ref[:, pl.ds(pl.multiple_of(ctx * rows, rows), rows)].astype(F32)
    for b in range(reach + 1):
        first = (ctx - (reach - b)) * rows
        from_row = pl.multiple_of(jnp.maximum(ctx - (reach - b), 0) * rows, rows)
        key_seg = jnp.broadcast_to(seg_ref[:, pl.ds(from_row, rows)].astype(F32), (rows, rows)).T
        key_pos = key_at + first
        gap = query_at - key_pos
        ok = (key_seg == query_seg) & (gap >= 0) & (gap < window) & (key_pos >= 0)
        ok = ok & ((key_pos < length) | (gap == 0))
        bias[pl.ds(b * rows, rows), :] = jnp.where(ok, 0.0, -1e30)
    live = (lax.broadcasted_iota(jnp.int32, (1, rows), 1) + ctx * rows < length).astype(F32)

    for off in range(1, reach + 1):
        slot = pl.ds((reach - off) * rows, rows)

        @pl.when(ctx - off < 0)
        def _():
            kbuf[slot, :] = jnp.zeros((rows, head), BF16)
            vbuf[slot, :] = jnp.zeros((rows, head), BF16)

    for copy in loads:
        copy.wait()
    for off in range(1, reach + 1):
        @pl.when(ctx - off >= 0)
        def _():
            for copy in kv_copies(off, ctx):
                copy.wait_recv()

    for h in range(group):
        if h == group // 2:
            issue(pieces[2:3])
        here = pl.ds(h * rows, rows)
        score = lax.dot_general(kbuf[...], qs[here, :], NT, preferred_element_type=F32) + bias[...]
        top = jnp.max(score, axis=0, keepdims=True)
        unnorm = jnp.exp2((score - top) * (scale * LOG2E))
        probs = unnorm * (live / jnp.sum(unnorm, axis=0, keepdims=True))
        p_low[:, here] = probs.astype(BF16)
        dprobs = lax.dot_general(vbuf[...], gos[here, :], NT, preferred_element_type=F32)
        row_dot = jnp.sum(probs * dprobs, axis=0, keepdims=True)
        ds_low[:, here] = (probs * (dprobs - row_dot)).astype(BF16)

    def kv_grad(b):
        block = pl.ds(b * rows, rows)
        gk = jnp.dot(ds_low[block, :], qs[...], preferred_element_type=F32) * scale
        gv = jnp.dot(p_low[block, :], gos[...], preferred_element_type=F32)
        return gk, gv

    def g_copy(off, to):
        return remote(gsend.at[off - 1], grecv.at[off - 1], g_ss.at[off - 1], g_rs.at[off - 1], dp, to)

    for off in range(1, reach + 1):
        gk, gv = kv_grad(reach - off)
        gsend[off - 1, :, pl.ds(0, head)] = gk.astype(BF16)
        gsend[off - 1, :, pl.ds(head, head)] = gv.astype(BF16)

        @pl.when(ctx - off >= 0)
        def _():
            g_copy(off, (ctx + n_ctx - off) % n_ctx).start()

        @pl.when(ctx + off >= n_ctx)
        def _():
            grecv[off - 1] = jnp.zeros((rows, 2 * head), BF16)

    issue(pieces[3:4])
    gk, gv = kv_grad(reach)

    key_t = kbuf[...].astype(F32).T.astype(BF16)
    for h in range(group):
        here = pl.ds(h * rows, rows)
        gq_t = jnp.dot(key_t, ds_low[:, here], preferred_element_type=F32) * scale
        gq_ref[:, pl.ds(h * head, head)] = gq_t.T.astype(BF16)

    for off in range(1, reach + 1):
        @pl.when(ctx + off < n_ctx)
        def _():
            g_copy(off, ctx).wait_recv()
    for off in range(1, reach + 1):
        gk = gk + grecv[off - 1, :, pl.ds(0, head)].astype(F32)
        gv = gv + grecv[off - 1, :, pl.ds(head, head)].astype(F32)
    own = pl.ds(pl.multiple_of(ctx * rows, rows), rows)
    gkv_t[pl.ds(0, head), own] = gk.T.astype(BF16)
    gkv_t[pl.ds(head, head), own] = gv.T.astype(BF16)

    def a_copy(o, source, to):
        part = gkv_t.at[:, pl.ds(pl.multiple_of(source * rows, rows), rows)]
        return remote(part, part, a_ss.at[o - 1], a_rs.at[o - 1], dp, to)

    for o in range(1, n_ctx):
        a_copy(o, ctx, (ctx + o) % n_ctx).start()
    issue(pieces[4:])
    for o in range(1, n_ctx):
        a_copy(o, (ctx + n_ctx - o) % n_ctx, ctx).wait_recv()

    def product(k, s):
        for o in range(1, n_ctx):
            x_copy(k, s, o, (ctx + n_ctx - o) % n_ctx, ctx).wait_recv()
        x_local(k, s).wait()
        return jnp.dot(gkv_t[...], xbuf[piece_dp(k, s)], preferred_element_type=F32)

    def c_copy(k):
        return remote(csend.at[k], crecv.at[k], c_ss.at[k], c_rs.at[k], sibling, ctx)

    def z_copy(k):
        return remote(zsend.at[k], zrecv.at[k], z_ss.at[k], z_rs.at[k], piece_dp(k, 1), ctx)

    def to_sibling(k):
        csend[k] = product(k, 0).astype(BF16)
        c_copy(k).start()

    total = None
    to_sibling(0)
    for k in range(nz):
        if k == 0:
            to_sibling(1)
        elif k > 1:
            to_sibling(k)
        part = product(k, 1)
        c_copy(k).wait_recv()
        part = part + crecv[k].astype(F32)
        if k < nz - 1:
            zsend[k] = part.astype(BF16)
            z_copy(k).start()
        else:
            total = part
    for k in range(nz - 1):
        z_copy(k).wait_recv()
        total = total + zrecv[k].astype(F32)
    gw_ref[...] = (total * (1.0 / n_dp)).T.astype(BF16)

    for off in range(1, reach + 1):
        @pl.when(ctx + off < n_ctx)
        def _():
            for copy in kv_copies(off, (ctx + off) % n_ctx):
                copy.wait_send()

        @pl.when(ctx - off >= 0)
        def _():
            g_copy(off, (ctx + n_ctx - off) % n_ctx).wait_send()
    for o in range(1, n_ctx):
        a_copy(o, ctx, (ctx + o) % n_ctx).wait_send()
    for k in range(nz):
        for s in range(2):
            for o in range(1, n_ctx):
                x_copy(k, s, o, ctx, (ctx + o) % n_ctx).wait_send()
        c_copy(k).wait_send()
        if k < nz - 1:
            z_copy(k).wait_send()


def hand_over(gq_from, gw_from, gq_to, gw_to):
    gq_to[...] = gq_from[...]
    gw_to[...] = gw_from[...]


def fused_shards(layer_input, queries, key_rows, value_rows, grad_output, segments, lengths):
    n_dp = lax.axis_size("dp")
    n_ctx = lax.axis_size("ctx")
    rows, width = layer_input.shape[1:]
    head = key_rows.shape[2]
    group = queries.shape[2] // head
    reach = min(8, n_ctx // 2)
    keys = (reach + 1) * rows
    slab = width // (n_dp * n_ctx)
    nz = n_dp // 2
    dma = pltpu.SemaphoreType.DMA
    hbm = pl.BlockSpec(memory_space=pltpu.HBM)
    vmem = pl.BlockSpec(memory_space=pltpu.VMEM)
    smem = pl.BlockSpec(memory_space=pltpu.SMEM)
    gq, gw = pl.pallas_call(
        functools.partial(fused_kernel, n_dp, n_ctx, reach),
        out_shape=(
            jax.ShapeDtypeStruct((rows, group * head), BF16),
            jax.ShapeDtypeStruct((slab, 2 * head), BF16),
        ),
        in_specs=[hbm] * 5 + [vmem, smem],
        out_specs=(vmem, vmem),
        scratch_shapes=[
            pltpu.VMEM((rows, width), BF16),
            pltpu.VMEM((keys, head), BF16),
            pltpu.VMEM((keys, head), BF16),
            pltpu.VMEM((group * rows, head), BF16),
            pltpu.VMEM((group * rows, head), BF16),
            pltpu.VMEM((keys, rows), F32),
            pltpu.VMEM((keys, group * rows), BF16),
            pltpu.VMEM((keys, group * rows), BF16),
            pltpu.VMEM((reach, rows, 2 * head), BF16),
            pltpu.VMEM((reach, rows, 2 * head), BF16),
            pltpu.VMEM((2 * head, n_ctx * rows), BF16),
            pltpu.VMEM((n_dp, n_ctx * rows, slab), BF16),
            pltpu.VMEM((nz, 2 * head, slab), BF16),
            pltpu.VMEM((nz, 2 * head, slab), BF16),
            pltpu.VMEM((nz - 1, 2 * head, slab), BF16),
            pltpu.VMEM((nz - 1, 2 * head, slab), BF16),
            dma((nz,)),
            dma((2 * group + 2,)),
            dma((nz, 2)),
            dma((reach, 2)),
            dma((reach, 2)),
            dma((reach,)),
            dma((reach,)),
            dma((n_ctx - 1,)),
            dma((n_ctx - 1,)),
            dma((nz, 2, n_ctx - 1)),
            dma((nz, 2, n_ctx - 1)),
            dma((nz,)),
            dma((nz,)),
            dma((nz - 1,)),
            dma((nz - 1,)),
        ],
        compiler_params=pltpu.CompilerParams(
            collective_id=0, has_side_effects=True, vmem_limit_bytes=62 * 1024 * 1024
        ),
    )(layer_input[0], queries[0], key_rows[0], value_rows[0], grad_output[0], segments, lengths)
    gq, gw = pl.pallas_call(
        hand_over,
        out_shape=(jax.ShapeDtypeStruct(gq.shape, BF16), jax.ShapeDtypeStruct(gw.shape, BF16)),
        in_specs=[vmem] * 2,
        out_specs=(vmem, vmem),
        compiler_params=pltpu.CompilerParams(vmem_limit_bytes=62 * 1024 * 1024),
    )(gq, gw)
    return gq[None], gw


def by_size(layer_input, *rest):
    n_dp, n_ctx = lax.axis_size("dp"), lax.axis_size("ctx")
    slab = layer_input.shape[2] // (n_dp * n_ctx)
    whole_tiles = slab % 128 == 0 and layer_input.shape[1] % 128 == 0
    run = fused_shards if whole_tiles and n_dp % 2 == 0 and n_dp > 2 else shards
    return run(layer_input, *rest)


def solution(mesh):
    return jax.shard_map(
        by_size,
        mesh=mesh,
        in_specs=(
            P("dp", "ctx", None),
            P("dp", "ctx", None),
            P("dp", "ctx", None),
            P("dp", "ctx", None),
            P("dp", "ctx", None),
            P("dp", None),
            P("dp"),
        ),
        out_specs=(P("dp", "ctx", None), P(("dp", "ctx"), None)),
        check_vma=False,
    )
```

```python
import functools
import math

import jax
import jax.numpy as jnp
from jax import lax
from jax.experimental import pallas as pl
from jax.experimental.pallas import tpu as pltpu
from jax.sharding import PartitionSpec as P

F32 = jnp.float32
BF16 = jnp.bfloat16
LOG2E = 1.4426950408889634
NT = (((1,), (1,)), ((), ()))


def passed_along(x, axis, by):
    length = lax.axis_size(axis)
    pairs = [(i, i + by) for i in range(length) if 0 <= i + by < length]
    return lax.ppermute(x, axis, pairs)


def make_mask(query_seg, key_seg, query_pos, key_pos, length, window_len):
    gap = query_pos[:, None] - key_pos[None, :]
    same_doc = query_seg[:, None] == key_seg[None, :]
    inside = (gap >= 0) & (gap < window_len)
    alive = (key_pos[None, :] < length) | (gap == 0)
    return same_doc & inside & alive


def block_grads(query_blk, upstream, key_all, allowed, live, score_scale):
    head_size = key_all.shape[1] // 2
    key_part = key_all[:, :head_size]
    value_part = key_all[:, head_size:]
    scores = (
        jnp.einsum("rgd,kd->grk", query_blk, key_part, preferred_element_type=jnp.float32)
        * score_scale
    )
    masked = jnp.where(allowed[None], scores, -1e30)
    row_max = jnp.max(masked, axis=2, keepdims=True)
    unnorm = jnp.where(allowed[None], jnp.exp(masked - row_max), 0.0)
    probs = unnorm / jnp.sum(unnorm, axis=2, keepdims=True) * live[None, :, None]
    probs_low = probs.astype(jnp.bfloat16)
    dprobs = jnp.einsum("rgd,kd->grk", upstream, value_part, preferred_element_type=jnp.float32)
    row_dot = jnp.sum(probs * dprobs, axis=2, keepdims=True)
    dscores = (probs * (dprobs - row_dot)).astype(jnp.bfloat16)
    grad_q = (
        jnp.einsum("grk,kd->rgd", dscores, key_part, preferred_element_type=jnp.float32)
        * score_scale
    ).astype(jnp.bfloat16)
    grad_k = (
        jnp.einsum("grk,rgd->kd", dscores, query_blk, preferred_element_type=jnp.float32)
        * score_scale
    )
    grad_v = jnp.einsum("grk,rgd->kd", probs_low, upstream, preferred_element_type=jnp.float32)
    return (grad_q.reshape(query_blk.shape[0], -1), jnp.concatenate([grad_k, grad_v], axis=1))


def shards(layer_input, queries, key_rows, value_rows, grad_output, segments, lengths):
    ctx_count = lax.axis_size("ctx")
    dp_count = lax.axis_size("dp")
    ctx_place = lax.axis_index("ctx")
    row_count = layer_input.shape[1]
    width_all = layer_input.shape[2]
    head_size = key_rows.shape[2]
    group_size = queries.shape[2] // head_size
    reach_count = min(8, ctx_count // 2)
    window_len = reach_count * row_count
    score_scale = 1.0 / math.sqrt(head_size)
    local_pair = jnp.concatenate([key_rows[0], value_rows[0]], axis=1)
    earlier = []
    for offset in range(1, reach_count + 1):
        earlier.append(passed_along(local_pair, "ctx", offset))
    key_all = jnp.concatenate(earlier[::-1] + [local_pair], axis=0)
    length = lengths[0]
    seg_row = segments[0]
    seg_pad = jnp.concatenate([jnp.full((window_len,), -1, jnp.int32), seg_row])
    first_row = ctx_place * row_count
    query_seg = lax.dynamic_slice_in_dim(seg_row, first_row, row_count, 0)
    key_seg = lax.dynamic_slice_in_dim(seg_pad, first_row, window_len + row_count, 0)
    query_pos = first_row + jnp.arange(row_count, dtype=jnp.int32)
    key_pos = first_row - window_len + jnp.arange(window_len + row_count, dtype=jnp.int32)
    allowed = make_mask(query_seg, key_seg, query_pos, key_pos, length, window_len)
    live = (query_pos < length).astype(jnp.float32)
    query_blk = queries[0].reshape(row_count, group_size, head_size)
    upstream = grad_output[0].reshape(row_count, group_size, head_size)
    grad_q, contrib = block_grads(query_blk, upstream, key_all, allowed, live, score_scale)
    blocks = contrib.reshape(reach_count + 1, row_count, 2 * head_size)
    total = blocks[reach_count]
    for offset in range(1, reach_count + 1):
        total = total + passed_along(blocks[reach_count - offset], "ctx", -offset)
    grad_kv = total.astype(jnp.bfloat16)
    slab_rows = width_all // (dp_count * ctx_count)
    inputs_flat = layer_input[0]
    partial_value = jnp.einsum(
        "rd,rc->dc", inputs_flat, grad_kv, preferred_element_type=jnp.float32
    )
    pieces = partial_value.reshape(dp_count, ctx_count, slab_rows, 2 * head_size)
    moved = lax.all_to_all(pieces, "ctx", split_axis=1, concat_axis=1, tiled=True)
    rollout_part = jnp.sum(moved, axis=1).reshape(dp_count * slab_rows, 2 * head_size)
    summed = lax.psum_scatter(rollout_part, "dp", scatter_dimension=0, tiled=True)
    grad_weights = (summed / dp_count).astype(jnp.bfloat16)
    return (grad_q.reshape(1, row_count, group_size * head_size), grad_weights)


def fused_kernel(
    n_dp, n_ctx, reach,
    x_ref, q_ref, k_ref, v_ref, go_ref, seg_ref, len_ref,
    gq_ref, gw_ref,
    xin, kbuf, vbuf, qs, gos, bias, p_low, ds_low, gsend, grecv, gkv_t, xbuf, csend, crecv, zsend, zrecv,
    xin_sem, load_sem, xl_sem, kv_ss, kv_rs, g_ss, g_rs, a_ss, a_rs, x_ss, x_rs, c_ss, c_rs, z_ss, z_rs,
):
    rows = k_ref.shape[0]
    head = k_ref.shape[1]
    group = q_ref.shape[1] // head
    slab = gw_ref.shape[0]
    nz = n_dp // 2
    window = reach * rows
    scale = 1.0 / math.sqrt(head)
    dp = lax.axis_index("dp")
    ctx = lax.axis_index("ctx")
    z = dp // 2
    core = dp % 2
    sibling = z * 2 + (1 - core)
    ny = n_ctx // 2
    row, col = ctx // 2, ctx % 2

    def peer_to(m):
        return ((row + m // 2) % ny) * 2 + (col + m % 2) % 2

    def peer_from(m):
        return ((row + ny - m // 2) % ny) * 2 + (col + m % 2) % 2


    def remote(src, dst, ss, rs, dp_to, ctx_to):
        return pltpu.make_async_remote_copy(
            src_ref=src, dst_ref=dst, send_sem=ss, recv_sem=rs,
            device_id={"dp": dp_to, "ctx": ctx_to}, device_id_type=pl.DeviceIdType.MESH,
        )

    loads = []
    for h in range(group):
        cols = pl.ds(h * head, head)
        loads.append(pltpu.make_async_copy(q_ref.at[:, cols], qs.at[pl.ds(h * rows, rows)], load_sem.at[2 * h]))
        loads.append(pltpu.make_async_copy(go_ref.at[:, cols], gos.at[pl.ds(h * rows, rows)], load_sem.at[2 * h + 1]))
    loads.append(pltpu.make_async_copy(k_ref, kbuf.at[pl.ds(window, rows)], load_sem.at[2 * group]))
    loads.append(pltpu.make_async_copy(v_ref, vbuf.at[pl.ds(window, rows)], load_sem.at[2 * group + 1]))
    for copy in loads:
        copy.start()

    def x_load(k):
        wide = 2 * n_ctx * slab
        cols = pl.ds(pl.multiple_of(((z + 1 + k) % nz) * wide, wide), wide)
        return pltpu.make_async_copy(x_ref.at[:, cols], xin.at[:, cols], xin_sem.at[k])

    for k in range(nz):
        x_load(k).start()

    barrier = pltpu.get_barrier_semaphore()
    for o in range(1, n_ctx):
        pl.semaphore_signal(barrier, inc=1, device_id={"dp": dp, "ctx": (ctx + o) % n_ctx}, device_id_type=pl.DeviceIdType.MESH)
    pl.semaphore_signal(barrier, inc=1, device_id={"dp": sibling, "ctx": ctx}, device_id_type=pl.DeviceIdType.MESH)
    for o in range(1, nz):
        pl.semaphore_signal(barrier, inc=1, device_id={"dp": ((z + o) % nz) * 2 + core, "ctx": ctx}, device_id_type=pl.DeviceIdType.MESH)
    pl.semaphore_wait(barrier, n_ctx - 1 + 1 + nz - 1)

    def kv_copies(off, to):
        slot = pl.ds((reach - off) * rows, rows)
        return (
            remote(k_ref, kbuf.at[slot], kv_ss.at[off - 1, 0], kv_rs.at[off - 1, 0], dp, to),
            remote(v_ref, vbuf.at[slot], kv_ss.at[off - 1, 1], kv_rs.at[off - 1, 1], dp, to),
        )

    for off in range(1, reach + 1):
        @pl.when(ctx + off < n_ctx)
        def _():
            for copy in kv_copies(off, (ctx + off) % n_ctx):
                copy.start()

    def piece_dp(k, s):
        return ((z + 1 + k) % nz) * 2 + (1 - core if s == 0 else core)

    def x_copy(k, s, o, source, to):
        d = piece_dp(k, s)
        cols = pl.ds(pl.multiple_of((d * n_ctx + to) * slab, slab), slab)
        return remote(
            xin.at[:, cols], xbuf.at[d, pl.ds(pl.multiple_of(source * rows, rows), rows)],
            x_ss.at[k, s, o - 1], x_rs.at[k, s, o - 1], dp, to,
        )

    def x_local(k, s):
        d = piece_dp(k, s)
        cols = pl.ds(pl.multiple_of((d * n_ctx + ctx) * slab, slab), slab)
        return pltpu.make_async_copy(
            xin.at[:, cols], xbuf.at[d, pl.ds(pl.multiple_of(ctx * rows, rows), rows)], xl_sem.at[k, s]
        )

    pieces = [(k, s) for k in range(nz) for s in range(2)]

    def issue(some):
        for k, s in some:
            if s == 0:
                x_load(k).wait()
            for j in range(n_ctx - 1):
                m = 1 + (j + core) % 2 if j < 2 else j + 1
                x_copy(k, s, m, ctx, peer_to(m)).start()
            x_local(k, s).start()

    issue(pieces[:2])

    length = len_ref[0]
    key_at = lax.broadcasted_iota(jnp.int32, (rows, rows), 0)
    query_at = lax.broadcasted_iota(jnp.int32, (rows, rows), 1) + ctx * rows
    query_seg = seg_ref[:, pl.ds(pl.multiple_of(ctx * rows, rows), rows)].astype(F32)
    for b in range(reach + 1):
        first = (ctx - (reach - b)) * rows
        from_row = pl.multiple_of(jnp.maximum(ctx - (reach - b), 0) * rows, rows)
        key_seg = jnp.broadcast_to(seg_ref[:, pl.ds(from_row, rows)].astype(F32), (rows, rows)).T
        key_pos = key_at + first
        gap = query_at - key_pos
        ok = (key_seg == query_seg) & (gap >= 0) & (gap < window) & (key_pos >= 0)
        ok = ok & ((key_pos < length) | (gap == 0))
        bias[pl.ds(b * rows, rows), :] = jnp.where(ok, 0.0, -1e30)
    live = (lax.broadcasted_iota(jnp.int32, (1, rows), 1) + ctx * rows < length).astype(F32)

    for off in range(1, reach + 1):
        slot = pl.ds((reach - off) * rows, rows)

        @pl.when(ctx - off < 0)
        def _():
            kbuf[slot, :] = jnp.zeros((rows, head), BF16)
            vbuf[slot, :] = jnp.zeros((rows, head), BF16)

    for copy in loads:
        copy.wait()
    for off in range(1, reach + 1):
        @pl.when(ctx - off >= 0)
        def _():
            for copy in kv_copies(off, ctx):
                copy.wait_recv()

    for h in range(group):
        if h == group // 2:
            issue(pieces[2:3])
        here = pl.ds(h * rows, rows)
        score = lax.dot_general(kbuf[...], qs[here, :], NT, preferred_element_type=F32) + bias[...]
        top = jnp.max(score, axis=0, keepdims=True)
        unnorm = jnp.exp2((score - top) * (scale * LOG2E))
        probs = unnorm * (live / jnp.sum(unnorm, axis=0, keepdims=True))
        p_low[:, here] = probs.astype(BF16)
        dprobs = lax.dot_general(vbuf[...], gos[here, :], NT, preferred_element_type=F32)
        row_dot = jnp.sum(probs * dprobs, axis=0, keepdims=True)
        ds_low[:, here] = (probs * (dprobs - row_dot)).astype(BF16)

    def kv_grad(b):
        block = pl.ds(b * rows, rows)
        gk = jnp.dot(ds_low[block, :], qs[...], preferred_element_type=F32) * scale
        gv = jnp.dot(p_low[block, :], gos[...], preferred_element_type=F32)
        return gk, gv

    def g_copy(off, to):
        return remote(gsend.at[off - 1], grecv.at[off - 1], g_ss.at[off - 1], g_rs.at[off - 1], dp, to)

    for off in range(1, reach + 1):
        gk, gv = kv_grad(reach - off)
        gsend[off - 1, :, pl.ds(0, head)] = gk.astype(BF16)
        gsend[off - 1, :, pl.ds(head, head)] = gv.astype(BF16)

        @pl.when(ctx - off >= 0)
        def _():
            g_copy(off, (ctx + n_ctx - off) % n_ctx).start()

        @pl.when(ctx + off >= n_ctx)
        def _():
            grecv[off - 1] = jnp.zeros((rows, 2 * head), BF16)

    issue(pieces[3:4])
    gk, gv = kv_grad(reach)

    key_t = kbuf[...].astype(F32).T.astype(BF16)
    for h in range(group):
        here = pl.ds(h * rows, rows)
        gq_t = jnp.dot(key_t, ds_low[:, here], preferred_element_type=F32) * scale
        gq_ref[:, pl.ds(h * head, head)] = gq_t.T.astype(BF16)

    for off in range(1, reach + 1):
        @pl.when(ctx + off < n_ctx)
        def _():
            g_copy(off, ctx).wait_recv()
    for off in range(1, reach + 1):
        gk = gk + grecv[off - 1, :, pl.ds(0, head)].astype(F32)
        gv = gv + grecv[off - 1, :, pl.ds(head, head)].astype(F32)
    own = pl.ds(pl.multiple_of(ctx * rows, rows), rows)
    gkv_t[pl.ds(0, head), own] = gk.T.astype(BF16)
    gkv_t[pl.ds(head, head), own] = gv.T.astype(BF16)

    def a_copy(o, source, to):
        part = gkv_t.at[:, pl.ds(pl.multiple_of(source * rows, rows), rows)]
        return remote(part, part, a_ss.at[o - 1], a_rs.at[o - 1], dp, to)

    for o in range(1, n_ctx):
        a_copy(o, ctx, peer_to(o)).start()
    issue(pieces[4:])
    for o in range(1, n_ctx):
        a_copy(o, peer_from(o), ctx).wait_recv()

    def product(k, s):
        for o in range(1, n_ctx):
            x_copy(k, s, o, peer_from(o), ctx).wait_recv()
        x_local(k, s).wait()
        return jnp.dot(gkv_t[...], xbuf[piece_dp(k, s)], preferred_element_type=F32)

    def c_copy(k):
        return remote(csend.at[k], crecv.at[k], c_ss.at[k], c_rs.at[k], sibling, ctx)

    def z_copy(k):
        return remote(zsend.at[k], zrecv.at[k], z_ss.at[k], z_rs.at[k], piece_dp(k, 1), ctx)

    def to_sibling(k):
        csend[k] = product(k, 0).astype(BF16)
        c_copy(k).start()

    total = None
    to_sibling(0)
    for k in range(nz):
        if k == 0:
            to_sibling(1)
        elif k > 1:
            to_sibling(k)
        part = product(k, 1)
        c_copy(k).wait_recv()
        part = part + crecv[k].astype(F32)
        if k < nz - 1:
            zsend[k] = part.astype(BF16)
            z_copy(k).start()
        else:
            total = part
    for k in range(nz - 1):
        z_copy(k).wait_recv()
        total = total + zrecv[k].astype(F32)
    gw_ref[...] = (total * (1.0 / n_dp)).T.astype(BF16)

    for off in range(1, reach + 1):
        @pl.when(ctx + off < n_ctx)
        def _():
            for copy in kv_copies(off, (ctx + off) % n_ctx):
                copy.wait_send()

        @pl.when(ctx - off >= 0)
        def _():
            g_copy(off, (ctx + n_ctx - off) % n_ctx).wait_send()
    for o in range(1, n_ctx):
        a_copy(o, ctx, peer_to(o)).wait_send()
    for k in range(nz):
        for s in range(2):
            for o in range(1, n_ctx):
                x_copy(k, s, o, ctx, peer_to(o)).wait_send()
        c_copy(k).wait_send()
        if k < nz - 1:
            z_copy(k).wait_send()


def hand_over(gq_from, gw_from, gq_to, gw_to):
    gq_to[...] = gq_from[...]
    gw_to[...] = gw_from[...]


def fused_shards(layer_input, queries, key_rows, value_rows, grad_output, segments, lengths):
    n_dp = lax.axis_size("dp")
    n_ctx = lax.axis_size("ctx")
    rows, width = layer_input.shape[1:]
    head = key_rows.shape[2]
    group = queries.shape[2] // head
    reach = min(8, n_ctx // 2)
    keys = (reach + 1) * rows
    slab = width // (n_dp * n_ctx)
    nz = n_dp // 2
    dma = pltpu.SemaphoreType.DMA
    hbm = pl.BlockSpec(memory_space=pltpu.HBM)
    vmem = pl.BlockSpec(memory_space=pltpu.VMEM)
    smem = pl.BlockSpec(memory_space=pltpu.SMEM)
    gq, gw = pl.pallas_call(
        functools.partial(fused_kernel, n_dp, n_ctx, reach),
        out_shape=(
            jax.ShapeDtypeStruct((rows, group * head), BF16),
            jax.ShapeDtypeStruct((slab, 2 * head), BF16),
        ),
        in_specs=[hbm] * 5 + [vmem, smem],
        out_specs=(vmem, vmem),
        scratch_shapes=[
            pltpu.VMEM((rows, width), BF16),
            pltpu.VMEM((keys, head), BF16),
            pltpu.VMEM((keys, head), BF16),
            pltpu.VMEM((group * rows, head), BF16),
            pltpu.VMEM((group * rows, head), BF16),
            pltpu.VMEM((keys, rows), F32),
            pltpu.VMEM((keys, group * rows), BF16),
            pltpu.VMEM((keys, group * rows), BF16),
            pltpu.VMEM((reach, rows, 2 * head), BF16),
            pltpu.VMEM((reach, rows, 2 * head), BF16),
            pltpu.VMEM((2 * head, n_ctx * rows), BF16),
            pltpu.VMEM((n_dp, n_ctx * rows, slab), BF16),
            pltpu.VMEM((nz, 2 * head, slab), BF16),
            pltpu.VMEM((nz, 2 * head, slab), BF16),
            pltpu.VMEM((nz - 1, 2 * head, slab), BF16),
            pltpu.VMEM((nz - 1, 2 * head, slab), BF16),
            dma((nz,)),
            dma((2 * group + 2,)),
            dma((nz, 2)),
            dma((reach, 2)),
            dma((reach, 2)),
            dma((reach,)),
            dma((reach,)),
            dma((n_ctx - 1,)),
            dma((n_ctx - 1,)),
            dma((nz, 2, n_ctx - 1)),
            dma((nz, 2, n_ctx - 1)),
            dma((nz,)),
            dma((nz,)),
            dma((nz - 1,)),
            dma((nz - 1,)),
        ],
        compiler_params=pltpu.CompilerParams(
            collective_id=0, has_side_effects=True, vmem_limit_bytes=62 * 1024 * 1024
        ),
    )(layer_input[0], queries[0], key_rows[0], value_rows[0], grad_output[0], segments, lengths)
    gq, gw = pl.pallas_call(
        hand_over,
        out_shape=(jax.ShapeDtypeStruct(gq.shape, BF16), jax.ShapeDtypeStruct(gw.shape, BF16)),
        in_specs=[vmem] * 2,
        out_specs=(vmem, vmem),
        compiler_params=pltpu.CompilerParams(vmem_limit_bytes=62 * 1024 * 1024),
    )(gq, gw)
    return gq[None], gw


def by_size(layer_input, *rest):
    n_dp, n_ctx = lax.axis_size("dp"), lax.axis_size("ctx")
    slab = layer_input.shape[2] // (n_dp * n_ctx)
    whole_tiles = slab % 128 == 0 and layer_input.shape[1] % 128 == 0
    run = fused_shards if whole_tiles and n_dp % 2 == 0 and n_ctx % 2 == 0 and min(n_dp, n_ctx) > 2 else shards
    return run(layer_input, *rest)


def solution(mesh):
    return jax.shard_map(
        by_size,
        mesh=mesh,
        in_specs=(
            P("dp", "ctx", None),
            P("dp", "ctx", None),
            P("dp", "ctx", None),
            P("dp", "ctx", None),
            P("dp", "ctx", None),
            P("dp", None),
            P("dp"),
        ),
        out_specs=(P("dp", "ctx", None), P(("dp", "ctx"), None)),
        check_vma=False,
    )
```

```python
import functools
import math

import jax
import jax.numpy as jnp
from jax import lax
from jax.experimental import pallas as pl
from jax.experimental.pallas import tpu as pltpu
from jax.sharding import PartitionSpec as P

F32 = jnp.float32
BF16 = jnp.bfloat16
LOG2E = 1.4426950408889634
NT = (((1,), (1,)), ((), ()))


def passed_along(x, axis, by):
    length = lax.axis_size(axis)
    pairs = [(i, i + by) for i in range(length) if 0 <= i + by < length]
    return lax.ppermute(x, axis, pairs)


def make_mask(query_seg, key_seg, query_pos, key_pos, length, window_len):
    gap = query_pos[:, None] - key_pos[None, :]
    same_doc = query_seg[:, None] == key_seg[None, :]
    inside = (gap >= 0) & (gap < window_len)
    alive = (key_pos[None, :] < length) | (gap == 0)
    return same_doc & inside & alive


def block_grads(query_blk, upstream, key_all, allowed, live, score_scale):
    head_size = key_all.shape[1] // 2
    key_part = key_all[:, :head_size]
    value_part = key_all[:, head_size:]
    scores = (
        jnp.einsum("rgd,kd->grk", query_blk, key_part, preferred_element_type=jnp.float32)
        * score_scale
    )
    masked = jnp.where(allowed[None], scores, -1e30)
    row_max = jnp.max(masked, axis=2, keepdims=True)
    unnorm = jnp.where(allowed[None], jnp.exp(masked - row_max), 0.0)
    probs = unnorm / jnp.sum(unnorm, axis=2, keepdims=True) * live[None, :, None]
    probs_low = probs.astype(jnp.bfloat16)
    dprobs = jnp.einsum("rgd,kd->grk", upstream, value_part, preferred_element_type=jnp.float32)
    row_dot = jnp.sum(probs * dprobs, axis=2, keepdims=True)
    dscores = (probs * (dprobs - row_dot)).astype(jnp.bfloat16)
    grad_q = (
        jnp.einsum("grk,kd->rgd", dscores, key_part, preferred_element_type=jnp.float32)
        * score_scale
    ).astype(jnp.bfloat16)
    grad_k = (
        jnp.einsum("grk,rgd->kd", dscores, query_blk, preferred_element_type=jnp.float32)
        * score_scale
    )
    grad_v = jnp.einsum("grk,rgd->kd", probs_low, upstream, preferred_element_type=jnp.float32)
    return (grad_q.reshape(query_blk.shape[0], -1), jnp.concatenate([grad_k, grad_v], axis=1))


def shards(layer_input, queries, key_rows, value_rows, grad_output, segments, lengths):
    ctx_count = lax.axis_size("ctx")
    dp_count = lax.axis_size("dp")
    ctx_place = lax.axis_index("ctx")
    row_count = layer_input.shape[1]
    width_all = layer_input.shape[2]
    head_size = key_rows.shape[2]
    group_size = queries.shape[2] // head_size
    reach_count = min(8, ctx_count // 2)
    window_len = reach_count * row_count
    score_scale = 1.0 / math.sqrt(head_size)
    local_pair = jnp.concatenate([key_rows[0], value_rows[0]], axis=1)
    earlier = []
    for offset in range(1, reach_count + 1):
        earlier.append(passed_along(local_pair, "ctx", offset))
    key_all = jnp.concatenate(earlier[::-1] + [local_pair], axis=0)
    length = lengths[0]
    seg_row = segments[0]
    seg_pad = jnp.concatenate([jnp.full((window_len,), -1, jnp.int32), seg_row])
    first_row = ctx_place * row_count
    query_seg = lax.dynamic_slice_in_dim(seg_row, first_row, row_count, 0)
    key_seg = lax.dynamic_slice_in_dim(seg_pad, first_row, window_len + row_count, 0)
    query_pos = first_row + jnp.arange(row_count, dtype=jnp.int32)
    key_pos = first_row - window_len + jnp.arange(window_len + row_count, dtype=jnp.int32)
    allowed = make_mask(query_seg, key_seg, query_pos, key_pos, length, window_len)
    live = (query_pos < length).astype(jnp.float32)
    query_blk = queries[0].reshape(row_count, group_size, head_size)
    upstream = grad_output[0].reshape(row_count, group_size, head_size)
    grad_q, contrib = block_grads(query_blk, upstream, key_all, allowed, live, score_scale)
    blocks = contrib.reshape(reach_count + 1, row_count, 2 * head_size)
    total = blocks[reach_count]
    for offset in range(1, reach_count + 1):
        total = total + passed_along(blocks[reach_count - offset], "ctx", -offset)
    grad_kv = total.astype(jnp.bfloat16)
    slab_rows = width_all // (dp_count * ctx_count)
    inputs_flat = layer_input[0]
    partial_value = jnp.einsum(
        "rd,rc->dc", inputs_flat, grad_kv, preferred_element_type=jnp.float32
    )
    pieces = partial_value.reshape(dp_count, ctx_count, slab_rows, 2 * head_size)
    moved = lax.all_to_all(pieces, "ctx", split_axis=1, concat_axis=1, tiled=True)
    rollout_part = jnp.sum(moved, axis=1).reshape(dp_count * slab_rows, 2 * head_size)
    summed = lax.psum_scatter(rollout_part, "dp", scatter_dimension=0, tiled=True)
    grad_weights = (summed / dp_count).astype(jnp.bfloat16)
    return (grad_q.reshape(1, row_count, group_size * head_size), grad_weights)


def fused_kernel(
    n_dp, n_ctx, reach,
    x_ref, q_ref, k_ref, v_ref, go_ref, seg_ref, len_ref,
    gq_ref, gw_ref,
    xin, kbuf, vbuf, qs, gos, bias, p_low, ds_low, gsend, grecv, gkv_t, xbuf, csend, crecv, zsend, zrecv,
    xin_sem, load_sem, xl_sem, kv_ss, kv_rs, g_ss, g_rs, a_ss, a_rs, x_ss, x_rs, c_ss, c_rs, z_ss, z_rs,
):
    rows = k_ref.shape[0]
    head = k_ref.shape[1]
    group = q_ref.shape[1] // head
    slab = gw_ref.shape[0]
    nz = n_dp // 2
    window = reach * rows
    scale = 1.0 / math.sqrt(head)
    dp = lax.axis_index("dp")
    ctx = lax.axis_index("ctx")
    z = dp // 2
    core = dp % 2
    sibling = z * 2 + (1 - core)
    ny = n_ctx // 2
    row, col = ctx // 2, ctx % 2

    def peer_to(m):
        return ((row + m // 2) % ny) * 2 + (col + m % 2) % 2

    def peer_from(m):
        return ((row + ny - m // 2) % ny) * 2 + (col + m % 2) % 2


    def remote(src, dst, ss, rs, dp_to, ctx_to):
        return pltpu.make_async_remote_copy(
            src_ref=src, dst_ref=dst, send_sem=ss, recv_sem=rs,
            device_id={"dp": dp_to, "ctx": ctx_to}, device_id_type=pl.DeviceIdType.MESH,
        )

    loads = []
    for h in range(group):
        cols = pl.ds(h * head, head)
        loads.append(pltpu.make_async_copy(q_ref.at[:, cols], qs.at[pl.ds(h * rows, rows)], load_sem.at[2 * h]))
        loads.append(pltpu.make_async_copy(go_ref.at[:, cols], gos.at[pl.ds(h * rows, rows)], load_sem.at[2 * h + 1]))
    loads.append(pltpu.make_async_copy(k_ref, kbuf.at[pl.ds(window, rows)], load_sem.at[2 * group]))
    loads.append(pltpu.make_async_copy(v_ref, vbuf.at[pl.ds(window, rows)], load_sem.at[2 * group + 1]))
    for copy in loads:
        copy.start()

    barrier = pltpu.get_barrier_semaphore()
    for o in range(1, n_ctx):
        pl.semaphore_signal(barrier, inc=1, device_id={"dp": dp, "ctx": (ctx + o) % n_ctx}, device_id_type=pl.DeviceIdType.MESH)
    pl.semaphore_signal(barrier, inc=1, device_id={"dp": sibling, "ctx": ctx}, device_id_type=pl.DeviceIdType.MESH)
    for o in range(1, nz):
        pl.semaphore_signal(barrier, inc=1, device_id={"dp": ((z + o) % nz) * 2 + core, "ctx": ctx}, device_id_type=pl.DeviceIdType.MESH)

    def piece_dp(k, s):
        return ((z + 1 + k) % nz) * 2 + (1 - core if s == 0 else core)

    def x_cols(d, to):
        return pl.ds(pl.multiple_of((d * n_ctx + to) * slab, slab), slab)

    def x_pack(k, s, m):
        d = piece_dp(k, s)
        return pltpu.make_async_copy(x_ref.at[:, x_cols(d, peer_to(m))], xin.at[d, peer_to(m)], xin_sem.at[k, s, m - 1])

    def x_local(k, s):
        d = piece_dp(k, s)
        mine = pl.ds(pl.multiple_of(ctx * rows, rows), rows)
        return pltpu.make_async_copy(x_ref.at[:, x_cols(d, ctx)], xbuf.at[d, mine], xl_sem.at[k, s])

    pieces = [(k, s) for k in range(nz) for s in range(2)]

    def pack(some):
        for k, s in some:
            for m in range(1, n_ctx):
                x_pack(k, s, m).start()
            x_local(k, s).start()

    pack(pieces[:2])
    pl.semaphore_wait(barrier, n_ctx - 1 + 1 + nz - 1)

    def kv_copies(off, to):
        slot = pl.ds((reach - off) * rows, rows)
        return (
            remote(k_ref, kbuf.at[slot], kv_ss.at[off - 1, 0], kv_rs.at[off - 1, 0], dp, to),
            remote(v_ref, vbuf.at[slot], kv_ss.at[off - 1, 1], kv_rs.at[off - 1, 1], dp, to),
        )

    for off in range(1, reach + 1):
        @pl.when(ctx + off < n_ctx)
        def _():
            for copy in kv_copies(off, (ctx + off) % n_ctx):
                copy.start()

    def x_copy(k, s, m, source, to):
        d = piece_dp(k, s)
        return remote(
            xin.at[d, to], xbuf.at[d, pl.ds(pl.multiple_of(source * rows, rows), rows)],
            x_ss.at[k, s, m - 1], x_rs.at[k, s, m - 1], dp, to,
        )

    def issue(some):
        for k, s in some:
            for m in range(1, n_ctx):
                x_pack(k, s, m).wait()
            for j in range(n_ctx - 1):
                m = 1 + (j + core) % 2 if j < 2 else j + 1
                x_copy(k, s, m, ctx, peer_to(m)).start()

    issue(pieces[:2])
    pack(pieces[2:])

    length = len_ref[0]
    key_at = lax.broadcasted_iota(jnp.int32, (rows, rows), 0)
    query_at = lax.broadcasted_iota(jnp.int32, (rows, rows), 1) + ctx * rows
    query_seg = seg_ref[:, pl.ds(pl.multiple_of(ctx * rows, rows), rows)].astype(F32)
    for b in range(reach + 1):
        first = (ctx - (reach - b)) * rows
        from_row = pl.multiple_of(jnp.maximum(ctx - (reach - b), 0) * rows, rows)
        key_seg = jnp.broadcast_to(seg_ref[:, pl.ds(from_row, rows)].astype(F32), (rows, rows)).T
        key_pos = key_at + first
        gap = query_at - key_pos
        ok = (key_seg == query_seg) & (gap >= 0) & (gap < window) & (key_pos >= 0)
        ok = ok & ((key_pos < length) | (gap == 0))
        bias[pl.ds(b * rows, rows), :] = jnp.where(ok, 0.0, -1e30)
    live = (lax.broadcasted_iota(jnp.int32, (1, rows), 1) + ctx * rows < length).astype(F32)

    for off in range(1, reach + 1):
        slot = pl.ds((reach - off) * rows, rows)

        @pl.when(ctx - off < 0)
        def _():
            kbuf[slot, :] = jnp.zeros((rows, head), BF16)
            vbuf[slot, :] = jnp.zeros((rows, head), BF16)

    for copy in loads:
        copy.wait()
    for off in range(1, reach + 1):
        @pl.when(ctx - off >= 0)
        def _():
            for copy in kv_copies(off, ctx):
                copy.wait_recv()

    for h in range(group):
        here = pl.ds(h * rows, rows)
        score = lax.dot_general(kbuf[...], qs[here, :], NT, preferred_element_type=F32) + bias[...]
        top = jnp.max(score, axis=0, keepdims=True)
        unnorm = jnp.exp2((score - top) * (scale * LOG2E))
        probs = unnorm * (live / jnp.sum(unnorm, axis=0, keepdims=True))
        p_low[:, here] = probs.astype(BF16)
        dprobs = lax.dot_general(vbuf[...], gos[here, :], NT, preferred_element_type=F32)
        row_dot = jnp.sum(probs * dprobs, axis=0, keepdims=True)
        ds_low[:, here] = (probs * (dprobs - row_dot)).astype(BF16)

    def kv_grad(b):
        block = pl.ds(b * rows, rows)
        gk = jnp.dot(ds_low[block, :], qs[...], preferred_element_type=F32) * scale
        gv = jnp.dot(p_low[block, :], gos[...], preferred_element_type=F32)
        return gk, gv

    def g_copy(off, to):
        return remote(gsend.at[off - 1], grecv.at[off - 1], g_ss.at[off - 1], g_rs.at[off - 1], dp, to)

    for off in range(1, reach + 1):
        gk, gv = kv_grad(reach - off)
        gsend[off - 1, :, pl.ds(0, head)] = gk.astype(BF16)
        gsend[off - 1, :, pl.ds(head, head)] = gv.astype(BF16)

        @pl.when(ctx - off >= 0)
        def _():
            g_copy(off, (ctx + n_ctx - off) % n_ctx).start()

        @pl.when(ctx + off >= n_ctx)
        def _():
            grecv[off - 1] = jnp.zeros((rows, 2 * head), BF16)

    issue(pieces[2:3])
    gk, gv = kv_grad(reach)

    key_t = kbuf[...].astype(F32).T.astype(BF16)
    for h in range(group):
        here = pl.ds(h * rows, rows)
        gq_t = jnp.dot(key_t, ds_low[:, here], preferred_element_type=F32) * scale
        gq_ref[:, pl.ds(h * head, head)] = gq_t.T.astype(BF16)

    for off in range(1, reach + 1):
        @pl.when(ctx + off < n_ctx)
        def _():
            g_copy(off, ctx).wait_recv()
    for off in range(1, reach + 1):
        gk = gk + grecv[off - 1, :, pl.ds(0, head)].astype(F32)
        gv = gv + grecv[off - 1, :, pl.ds(head, head)].astype(F32)
    own = pl.ds(pl.multiple_of(ctx * rows, rows), rows)
    gkv_t[pl.ds(0, head), own] = gk.T.astype(BF16)
    gkv_t[pl.ds(head, head), own] = gv.T.astype(BF16)

    def a_copy(o, source, to):
        part = gkv_t.at[:, pl.ds(pl.multiple_of(source * rows, rows), rows)]
        return remote(part, part, a_ss.at[o - 1], a_rs.at[o - 1], dp, to)

    for o in range(1, n_ctx):
        a_copy(o, ctx, peer_to(o)).start()
    issue(pieces[3:])
    for o in range(1, n_ctx):
        a_copy(o, peer_from(o), ctx).wait_recv()

    def product(k, s):
        for o in range(1, n_ctx):
            x_copy(k, s, o, peer_from(o), ctx).wait_recv()
        x_local(k, s).wait()
        return jnp.dot(gkv_t[...], xbuf[piece_dp(k, s)], preferred_element_type=F32)

    def c_copy(k):
        return remote(csend.at[k], crecv.at[k], c_ss.at[k], c_rs.at[k], sibling, ctx)

    def z_copy(k):
        return remote(zsend.at[k], zrecv.at[k], z_ss.at[k], z_rs.at[k], piece_dp(k, 1), ctx)

    def to_sibling(k):
        csend[k] = product(k, 0).astype(BF16)
        c_copy(k).start()

    total = None
    to_sibling(0)
    for k in range(nz):
        if k == 0:
            to_sibling(1)
        elif k > 1:
            to_sibling(k)
        part = product(k, 1)
        c_copy(k).wait_recv()
        part = part + crecv[k].astype(F32)
        if k < nz - 1:
            zsend[k] = part.astype(BF16)
            z_copy(k).start()
        else:
            total = part
    for k in range(nz - 1):
        z_copy(k).wait_recv()
        total = total + zrecv[k].astype(F32)
    gw_ref[...] = (total * (1.0 / n_dp)).T.astype(BF16)

    for off in range(1, reach + 1):
        @pl.when(ctx + off < n_ctx)
        def _():
            for copy in kv_copies(off, (ctx + off) % n_ctx):
                copy.wait_send()

        @pl.when(ctx - off >= 0)
        def _():
            g_copy(off, (ctx + n_ctx - off) % n_ctx).wait_send()
    for o in range(1, n_ctx):
        a_copy(o, ctx, peer_to(o)).wait_send()
    for k in range(nz):
        for s in range(2):
            for o in range(1, n_ctx):
                x_copy(k, s, o, ctx, peer_to(o)).wait_send()
        c_copy(k).wait_send()
        if k < nz - 1:
            z_copy(k).wait_send()


def hand_over(gq_from, gw_from, gq_to, gw_to):
    gq_to[...] = gq_from[...]
    gw_to[...] = gw_from[...]


def fused_shards(layer_input, queries, key_rows, value_rows, grad_output, segments, lengths):
    n_dp = lax.axis_size("dp")
    n_ctx = lax.axis_size("ctx")
    rows, width = layer_input.shape[1:]
    head = key_rows.shape[2]
    group = queries.shape[2] // head
    reach = min(8, n_ctx // 2)
    keys = (reach + 1) * rows
    slab = width // (n_dp * n_ctx)
    nz = n_dp // 2
    dma = pltpu.SemaphoreType.DMA
    hbm = pl.BlockSpec(memory_space=pltpu.HBM)
    vmem = pl.BlockSpec(memory_space=pltpu.VMEM)
    smem = pl.BlockSpec(memory_space=pltpu.SMEM)
    gq, gw = pl.pallas_call(
        functools.partial(fused_kernel, n_dp, n_ctx, reach),
        out_shape=(
            jax.ShapeDtypeStruct((rows, group * head), BF16),
            jax.ShapeDtypeStruct((slab, 2 * head), BF16),
        ),
        in_specs=[hbm] * 5 + [vmem, smem],
        out_specs=(vmem, vmem),
        scratch_shapes=[
            pltpu.VMEM((n_dp, n_ctx, rows, slab), BF16),
            pltpu.VMEM((keys, head), BF16),
            pltpu.VMEM((keys, head), BF16),
            pltpu.VMEM((group * rows, head), BF16),
            pltpu.VMEM((group * rows, head), BF16),
            pltpu.VMEM((keys, rows), F32),
            pltpu.VMEM((keys, group * rows), BF16),
            pltpu.VMEM((keys, group * rows), BF16),
            pltpu.VMEM((reach, rows, 2 * head), BF16),
            pltpu.VMEM((reach, rows, 2 * head), BF16),
            pltpu.VMEM((2 * head, n_ctx * rows), BF16),
            pltpu.VMEM((n_dp, n_ctx * rows, slab), BF16),
            pltpu.VMEM((nz, 2 * head, slab), BF16),
            pltpu.VMEM((nz, 2 * head, slab), BF16),
            pltpu.VMEM((nz - 1, 2 * head, slab), BF16),
            pltpu.VMEM((nz - 1, 2 * head, slab), BF16),
            dma((nz, 2, n_ctx - 1)),
            dma((2 * group + 2,)),
            dma((nz, 2)),
            dma((reach, 2)),
            dma((reach, 2)),
            dma((reach,)),
            dma((reach,)),
            dma((n_ctx - 1,)),
            dma((n_ctx - 1,)),
            dma((nz, 2, n_ctx - 1)),
            dma((nz, 2, n_ctx - 1)),
            dma((nz,)),
            dma((nz,)),
            dma((nz - 1,)),
            dma((nz - 1,)),
        ],
        compiler_params=pltpu.CompilerParams(
            collective_id=0, has_side_effects=True, vmem_limit_bytes=62 * 1024 * 1024
        ),
    )(layer_input[0], queries[0], key_rows[0], value_rows[0], grad_output[0], segments, lengths)
    gq, gw = pl.pallas_call(
        hand_over,
        out_shape=(jax.ShapeDtypeStruct(gq.shape, BF16), jax.ShapeDtypeStruct(gw.shape, BF16)),
        in_specs=[vmem] * 2,
        out_specs=(vmem, vmem),
        compiler_params=pltpu.CompilerParams(vmem_limit_bytes=62 * 1024 * 1024),
    )(gq, gw)
    return gq[None], gw


def by_size(layer_input, *rest):
    n_dp, n_ctx = lax.axis_size("dp"), lax.axis_size("ctx")
    slab = layer_input.shape[2] // (n_dp * n_ctx)
    whole_tiles = slab % 128 == 0 and layer_input.shape[1] % 128 == 0
    run = fused_shards if whole_tiles and n_dp % 2 == 0 and n_ctx % 2 == 0 and min(n_dp, n_ctx) > 2 else shards
    return run(layer_input, *rest)


def solution(mesh):
    return jax.shard_map(
        by_size,
        mesh=mesh,
        in_specs=(
            P("dp", "ctx", None),
            P("dp", "ctx", None),
            P("dp", "ctx", None),
            P("dp", "ctx", None),
            P("dp", "ctx", None),
            P("dp", None),
            P("dp"),
        ),
        out_specs=(P("dp", "ctx", None), P(("dp", "ctx"), None)),
        check_vma=False,
    )
```
